512 devices in a mesh: blk: 16 (over x, z_hi), shard: 32 (over y, z_lo, core).
Axes of the slice: x: 4, y: 8, z: 8 (z_hi: 4, z_lo: 2; z = z_hi * 2 + z_lo), core: 2. Of those that a mesh axis runs over, the one named last changes fastest.
Arguments:
- queries: bfloat16 [2048, 1280], P('blk'), may hold values from -56 to 56
- database: bfloat16 [393216, 1280], P(('blk', 'shard')), may hold values from -56 to 56
- pair_tiles: int32 [512, 24, 2], P(('blk', 'shard')), may hold values from 0 to 15, as said below
- pair_lengths: int32 [512, 24, 2], P(('blk', 'shard')), may hold values from 8 to 128
- live_pairs: int32 [512], P(('blk', 'shard')), may hold values from 1 to 24, as said below
Outputs:
- aligned: bfloat16 [2048, 1280], P(('blk', 'shard'))
The draws below stay inside these ranges and needn't reach their ends.
Inputs may be any that keep to these rules, and one draw needn't show every extreme that they name: `pair_tiles`: entry [e, p, 0] is a query tile in 0 to 15 and entry [e, p, 1] a tile of device e in 0 to 5; in each device's used slots the query tiles never fall. `live_pairs`: some device uses all 24 slots in every draw.
All inputs are finite; a program needn't handle non-finite values.
Results may differ from the reference program's by a relative error of at most 0.0055.
Values may be sent and summed in bfloat16 or wider, within the bound.
No kernel may reach another device: no remote copies, remote signals or barrier semaphores. Data moves between devices by JAX's collectives and lax.ppermute only.
A program may use at most 128 MiB of HBM per device.

```python
import jax
import jax.numpy as jnp
from jax import lax

D = 1280
TILE = 128
DBT_DEV = 6
PAIRS_DEV = 24
N_BLK = 16
N_SHARD = 32


def draw_queries(key, part):
    key = jax.random.fold_in(key, 11)
    second_key = jax.random.fold_in(key, 1)
    total_rows = N_BLK * TILE
    values = jnp.clip(jax.random.normal(second_key, (total_rows, D), jnp.float32), -6.0, 6.0)
    return values.astype(jnp.bfloat16)


def draw_database(key, part):
    key = jax.random.fold_in(key, 23)
    second_key = jax.random.fold_in(key, 1)
    total_rows = DBT_DEV * TILE * N_BLK * N_SHARD
    values = jnp.clip(jax.random.normal(second_key, (total_rows, D), jnp.float32), -6.0, 6.0)
    return values.astype(jnp.bfloat16)


def draw_plan(key):
    key = jax.random.fold_in(key, 5)
    first_key, second_key, third_key = jax.random.split(key, 3)
    devices = N_BLK * N_SHARD
    divisor = 1 + jax.random.randint(first_key, (devices,), 0, 4)
    live_count = jnp.maximum(PAIRS_DEV // divisor, 1).at[0].set(PAIRS_DEV).astype(jnp.int32)
    query_tile = jax.random.randint(second_key, (devices, PAIRS_DEV), 0, N_BLK)
    base_tile = jax.random.randint(third_key, (devices, PAIRS_DEV), 0, DBT_DEV)
    slots = jnp.arange(PAIRS_DEV)[None, :]
    sort_key = jnp.where(slots < live_count[:, None], query_tile, query_tile + N_BLK)
    ordering = jnp.argsort(sort_key, axis=1, stable=True)
    query_tile = jnp.take_along_axis(query_tile, ordering, axis=1)
    return (live_count, jnp.stack([query_tile, base_tile], axis=-1).astype(jnp.int32))


def draw_pair_tiles(key, part):
    return draw_plan(key)[1]


def draw_live_pairs(key, part):
    return draw_plan(key)[0]


def touch_ends(array, own_key, low, high):
    index_at = [jax.random.randint(jax.random.fold_in(own_key, axis), (), 0, length) for axis, length in enumerate(array.shape)]
    longest = array.shape.index(max(array.shape))
    beside = index_at[:longest] + [(index_at[longest] + 1) % array.shape[longest]] + index_at[longest + 1:]
    return array.at[tuple(index_at)].set(low).at[tuple(beside)].set(high)


def setup_inputs(seed: int = 0) -> dict:
    splits = jax.random.split(jax.random.key(seed), 6)
    return {
        "queries": draw_queries(jax.random.fold_in(splits[5], 71), 0),
        "database": draw_database(jax.random.fold_in(splits[5], 71), 0),
        "pair_tiles": draw_pair_tiles(jax.random.fold_in(splits[5], 71), 0),
        "pair_lengths": touch_ends(jax.random.randint(splits[3], (N_BLK * N_SHARD, PAIRS_DEV, 2), 8, TILE + 1), jax.random.fold_in(splits[3], 1), 8, TILE).astype(jnp.int32),
        "live_pairs": draw_live_pairs(jax.random.fold_in(splits[5], 71), 0),
    }


def pair_block(query_rows, key_rows, lengths):
    scores = jnp.einsum("pid,pjd->pij", query_rows.astype(jnp.float32), key_rows.astype(jnp.float32)) * (D ** -0.5)
    index = jnp.arange(TILE)
    valid = (index[None, :, None] < lengths[:, 0][:, None, None]) & (index[None, None, :] < lengths[:, 1][:, None, None])
    masked = jnp.where(valid, scores, -1e30)
    row_max = jnp.max(masked, axis=2, keepdims=True)
    row_lse = row_max + jnp.log(jnp.sum(jnp.exp(masked - row_max), axis=2, keepdims=True))
    col_max = jnp.max(masked, axis=1, keepdims=True)
    col_lse = col_max + jnp.log(jnp.sum(jnp.exp(masked - col_max), axis=1, keepdims=True))
    weight = jnp.where(valid, jnp.exp(scores - 0.5 * (row_lse + col_lse)), 0.0).astype(jnp.bfloat16)
    return jnp.einsum("pij,pjd->pid", weight.astype(jnp.float32), key_rows.astype(jnp.float32))


def reference(queries, database, pair_tiles, pair_lengths, live_pairs):
    devices = N_BLK * N_SHARD
    query_tiles = queries.reshape(N_BLK, TILE, D)
    own_tiles = database.reshape(devices, DBT_DEV, TILE, D)
    slots = jnp.arange(PAIRS_DEV)

    def one_device(total, device):
        listed = pair_tiles[device]
        query_rows = query_tiles[listed[:, 0]]
        key_rows = own_tiles[device][listed[:, 1]]
        terms = pair_block(query_rows, key_rows, pair_lengths[device])
        used = (slots < live_pairs[device]).astype(jnp.float32)
        onehot = (listed[:, 0][:, None] == jnp.arange(N_BLK)[None, :]).astype(jnp.float32) * used[:, None]
        return total + jnp.einsum("pq,pid->qid", onehot, terms), None

    start = jnp.zeros((N_BLK, TILE, D), jnp.float32)
    total, unused = lax.scan(one_device, start, jnp.arange(devices, dtype=jnp.int32))
    return total.reshape(N_BLK * TILE, D).astype(jnp.bfloat16)
```

```python
import functools

import jax
import jax.numpy as jnp
from jax import lax
from jax.experimental import pallas as pl
from jax.experimental.pallas import tpu as pltpu
from jax.sharding import Mesh
from jax.sharding import PartitionSpec as P

TILE = 128
BLK = ("x", "zh")
SHARD = ("y", "zl", "c")
GROUP_TILES = 2
UNROLL = 4


def pair_weight(scores, rows, cols, row_count, col_count):
    valid = (rows < row_count) & (cols < col_count)
    masked = jnp.where(valid, scores, -1e30)
    row_max = jnp.max(masked, axis=1, keepdims=True)
    row_lse = row_max + jnp.log(jnp.sum(jnp.exp(masked - row_max), axis=1, keepdims=True))
    col_max = jnp.max(masked, axis=0, keepdims=True)
    col_lse = col_max + jnp.log(jnp.sum(jnp.exp(masked - col_max), axis=0, keepdims=True))
    weight = jnp.where(valid, jnp.exp(scores - 0.5 * (row_lse + col_lse)), 0.0)
    return weight.astype(jnp.bfloat16)


def align_kernel(
    scale, tiles, slots, meta, q_ref, own_ref, other_ref, out_ref, scores, weights, listed, seen
):
    step = pl.program_id(0)
    width = tiles * TILE
    stride = meta.shape[0] // 2
    core = meta[4 * slots + 1]

    @pl.when(step == 0)
    def _():
        seen[0] = 0
        seen[1] = 0

    across = (((1,), (1,)), ((), ()))
    query = q_ref[...]
    for side, ref in enumerate((own_ref, other_ref)):
        scores[:, side * width : (side + 1) * width] = (
            lax.dot_general(query, ref[...], across, preferred_element_type=jnp.float32) * scale
        )
    weights[...] = jnp.zeros_like(weights)

    count = jnp.int32(0)
    for side in range(2):
        base = side * stride
        live = meta[base + 4 * slots]

        def here(slot, base=base, live=live):
            at = base + 2 * jnp.minimum(slot, slots - 1)
            return (slot < live) & ((meta[at] >> 2) == step)

        def take(carry, base=base, side=side):
            slot, count = carry
            query_tile = meta[base + 2 * slot]
            mine = (query_tile & 1) == core

            @pl.when(mine)
            def _():
                listed[0, count] = (query_tile & 3) >> 1
                listed[1, count] = meta[base + 2 * slot + 1] + side * tiles
                listed[2, count] = meta[base + 2 * slots + 2 * slot]
                listed[3, count] = meta[base + 2 * slots + 2 * slot + 1]

            return slot + 1, count + mine.astype(jnp.int32)

        slot, count = lax.while_loop(lambda carry: here(carry[0]), take, (seen[side], count))
        seen[side] = slot
    for extra in range(UNROLL - 1):
        listed[0, count + extra] = 0
        listed[1, count + extra] = 0
        listed[2, count + extra] = 0
        listed[3, count + extra] = 0

    place = lax.broadcasted_iota(jnp.int32, (TILE, TILE), 0)
    rows = ((place & 63) >> 2) * 8 + (place >> 6) * 4 + (place & 3)
    cols = lax.broadcasted_iota(jnp.int32, (TILE, TILE), 1)

    def batch(index, carry):
        made = []
        for k in range(UNROLL):
            slot = index * UNROLL + k
            at_row = pl.ds(pl.multiple_of(listed[0, slot] * TILE, TILE), TILE)
            at_col = pl.ds(pl.multiple_of(listed[1, slot] * TILE, TILE), TILE)
            weight = pair_weight(scores[at_row, at_col], rows, cols, listed[2, slot], listed[3, slot])
            made.append((at_row, at_col, weight))
        for at_row, at_col, weight in made:
            weights[at_row, at_col] += weight.astype(jnp.float32)
        return carry

    lax.fori_loop(0, (count + UNROLL - 1) // UNROLL, batch, 0)

    weight = weights[...].astype(jnp.bfloat16)
    out_ref[...] = (
        jnp.dot(weight[:, :width], own_ref[...], preferred_element_type=jnp.float32)
        + jnp.dot(weight[:, width:], other_ref[...], preferred_element_type=jnp.float32)
    ).astype(out_ref.dtype)


def align(meta, queries, own, other, slots):
    rows, width = queries.shape
    block = GROUP_TILES * TILE
    tiles = own.shape[0] // TILE
    columns = 2 * own.shape[0]
    whole = pl.BlockSpec(own.shape, lambda i, meta: (0, 0))
    return pl.pallas_call(
        functools.partial(align_kernel, width ** (-0.5), tiles, slots),
        grid_spec=pltpu.PrefetchScalarGridSpec(
            num_scalar_prefetch=1,
            grid=(rows // block,),
            in_specs=[pl.BlockSpec((block, width), lambda i, meta: (i, 0)), whole, whole],
            out_specs=pl.BlockSpec((block, width), lambda i, meta: (i, 0)),
            scratch_shapes=[
                pltpu.VMEM((block, columns), jnp.float32),
                pltpu.VMEM((block, columns), jnp.float32),
                pltpu.SMEM((4, 2 * slots + UNROLL), jnp.int32),
                pltpu.SMEM((2,), jnp.int32),
            ],
        ),
        out_shape=jax.ShapeDtypeStruct((rows, width), jnp.bfloat16),
        compiler_params=pltpu.CompilerParams(
            dimension_semantics=("arbitrary",), vmem_limit_bytes=40 * 1024 * 1024
        ),
        cost_estimate=pl.CostEstimate(
            flops=4 * rows * columns * width, bytes_accessed=12 * 1024 * 1024, transcendentals=0
        ),
        name="align",
    )(meta, queries, own, other)


def sibling(value):
    return lax.ppermute(value, "c", [(0, 1), (1, 0)])


def on_device(queries, database, pair_tiles, pair_lengths, live_pairs):
    tile, width = queries.shape
    slots = pair_tiles.shape[1]
    core = lax.axis_index("c")
    groups = lax.axis_size("x")
    deep = lax.axis_size("zh")

    used = 4 * slots + 2
    own_meta = jnp.concatenate(
        [pair_tiles.reshape(-1), pair_lengths.reshape(-1), live_pairs, core[None].astype(jnp.int32)]
    )
    own_meta = jnp.pad(own_meta, (0, 128 - used))
    other_meta = sibling(own_meta)
    meta = jnp.concatenate([own_meta, other_meta])
    other = sibling(database)

    halves = queries.reshape(tile // 8, 2, 4, width).swapaxes(0, 1).reshape(2, tile // 2, width)
    half = lax.dynamic_index_in_dim(halves, core, 0, keepdims=False)

    column = lax.all_to_all(
        jnp.broadcast_to(half[None], (deep, tile // 2, width)), "zh", 0, 0, tiled=True
    ).reshape(deep // 2, 2, tile // 2, width)
    kept = lax.dynamic_index_in_dim(column, core, 1, keepdims=False)
    given = lax.dynamic_index_in_dim(column, 1 - core, 1, keepdims=False)
    taken = sibling(given)
    panel = jnp.where(
        core == 0, jnp.stack([kept, taken], 1), jnp.stack([taken, kept], 1)
    ).reshape(deep // 2 * tile, width)

    rows = panel.shape[0]
    panels = lax.all_to_all(
        jnp.broadcast_to(panel[None], (groups, rows, width)), "x", 0, 0, tiled=True
    ).reshape(groups * rows, width)

    terms = align(meta, panels, database, other, slots)

    parts = lax.all_to_all(terms.reshape(groups, rows, width), "x", 0, 0, tiled=True)
    summed = jnp.sum(parts.astype(jnp.float32), axis=0).astype(jnp.bfloat16)
    summed = summed.reshape(deep // 2, 2, tile // 2, width)
    kept = lax.dynamic_index_in_dim(summed, core, 1, keepdims=False)
    given = lax.dynamic_index_in_dim(summed, 1 - core, 1, keepdims=False)
    taken = sibling(given)
    column = jnp.where(core == 0, jnp.stack([kept, taken], 1), jnp.stack([taken, kept], 1))
    rest = ("zh", "y", "zl")
    pieces = lax.all_to_all(column.reshape(-1, 4, width), rest, 0, 0, tiled=True)
    return jnp.sum(pieces.astype(jnp.float32), axis=0).astype(jnp.bfloat16)


def solution(mesh):
    fine = Mesh(mesh.devices.reshape(4, 4, 8, 2, 2), BLK + SHARD)
    both = BLK + SHARD
    in_specs = (P(BLK, None), P(both, None), P(both, None, None), P(both, None, None), P(both))
    return jax.shard_map(
        on_device, mesh=fine, in_specs=in_specs, out_specs=P(both, None), check_vma=False
    )
```

```python
import functools

import jax
import jax.numpy as jnp
from jax import lax
from jax.experimental import pallas as pl
from jax.experimental.pallas import tpu as pltpu
from jax.sharding import Mesh
from jax.sharding import PartitionSpec as P

TILE = 128
BLK = ("x", "zh")
SHARD = ("y", "zl", "c")
HALF = 2
CHUNK = 256
UNROLL = 4


def pair_weight(scores, rows, cols, row_count, col_count):
    valid = (rows < row_count) & (cols < col_count)
    masked = jnp.where(valid, scores, -1e30)
    row_max = jnp.max(masked, axis=1, keepdims=True)
    row_lse = row_max + jnp.log(jnp.sum(jnp.exp(masked - row_max), axis=1, keepdims=True))
    col_max = jnp.max(masked, axis=0, keepdims=True)
    col_lse = col_max + jnp.log(jnp.sum(jnp.exp(masked - col_max), axis=0, keepdims=True))
    weight = jnp.where(valid, jnp.exp(scores - 0.5 * (row_lse + col_lse)), 0.0)
    return weight.astype(jnp.bfloat16)


def align_kernel(
    scale, tiles, slots, meta, group, q_ref, own_ref, other_ref, out_ref,
    base_rows, scores, weights, listed, arrived,
):
    stride = meta.shape[0] // 2
    core = meta[4 * slots + 1]
    deep = meta[4 * slots + 2]
    width = tiles * TILE
    chunks = 2 * width // CHUNK

    def copy(index):
        source = own_ref if index < chunks // 2 else other_ref
        first = (index % (chunks // 2)) * CHUNK
        return pltpu.make_async_copy(
            source.at[pl.ds(first, CHUNK)],
            base_rows.at[pl.ds(index * CHUNK, CHUNK)],
            arrived.at[index],
        )

    for index in range(chunks):
        copy(index).start()
    weights[...] = jnp.zeros_like(weights)

    count = jnp.int32(0)
    for side in range(2):
        base = side * stride

        def look(slot, count, base=base, side=side):
            query_tile = meta[base + 2 * slot]
            near = (query_tile & 3) ^ deep
            mine = ((query_tile >> 2) == group[0]) & ((near >> 1) == core)

            @pl.when(mine)
            def _():
                listed[0, count] = near & 1
                listed[1, count] = meta[base + 2 * slot + 1] + side * tiles
                listed[2, count] = meta[base + 2 * slots + 2 * slot]
                listed[3, count] = meta[base + 2 * slots + 2 * slot + 1]

            return count + mine.astype(jnp.int32)

        count = lax.fori_loop(0, meta[base + 4 * slots], look, count)
    for extra in range(UNROLL - 1):
        for field in range(4):
            listed[field, count + extra] = 0

    across = (((1,), (1,)), ((), ()))
    query = q_ref[...]
    for index in range(chunks):
        copy(index).wait()
        span = pl.ds(index * CHUNK, CHUNK)
        scores[:, span] = (
            lax.dot_general(
                query, base_rows[span, :], across, preferred_element_type=jnp.float32
            )
            * scale
        )

    rows = lax.broadcasted_iota(jnp.int32, (TILE, TILE), 0)
    cols = lax.broadcasted_iota(jnp.int32, (TILE, TILE), 1)

    def batch(index, carry):
        made = []
        for k in range(UNROLL):
            slot = index * UNROLL + k
            at_row = pl.ds(pl.multiple_of(listed[0, slot] * TILE, TILE), TILE)
            at_col = pl.ds(pl.multiple_of(listed[1, slot] * TILE, TILE), TILE)
            weight = pair_weight(scores[at_row, at_col], rows, cols, listed[2, slot], listed[3, slot])
            made.append((at_row, at_col, weight))
        for at_row, at_col, weight in made:
            weights[at_row, at_col] += weight.astype(jnp.float32)
        return carry

    lax.fori_loop(0, (count + UNROLL - 1) // UNROLL, batch, 0)

    both = HALF * TILE
    place = lax.broadcasted_iota(jnp.int32, (both, both), 0)
    row = lax.broadcasted_iota(jnp.int32, (both, both), 1)
    wanted = (place & ~127) + ((place & 63) >> 2) * 8 + ((place >> 6) & 1) * 4 + (place & 3)
    sort = (row == wanted).astype(jnp.bfloat16)
    weight = jnp.dot(
        sort, weights[...].astype(jnp.bfloat16), preferred_element_type=jnp.float32
    ).astype(jnp.bfloat16)
    out_ref[...] = jnp.dot(
        weight, base_rows[...], preferred_element_type=jnp.float32
    ).astype(out_ref.dtype)


def align(meta, group, queries, own, other, slots):
    rows, width = queries.shape
    tiles = own.shape[0] // TILE
    columns = 2 * own.shape[0]
    whole = pl.BlockSpec(memory_space=pl.ANY)
    block = pl.BlockSpec((rows, width), lambda i, meta, group: (0, 0))
    return pl.pallas_call(
        functools.partial(align_kernel, width ** (-0.5), tiles, slots),
        grid_spec=pltpu.PrefetchScalarGridSpec(
            num_scalar_prefetch=2,
            grid=(1,),
            in_specs=[block, whole, whole],
            out_specs=block,
            scratch_shapes=[
                pltpu.VMEM((columns, width), jnp.bfloat16),
                pltpu.VMEM((rows, columns), jnp.float32),
                pltpu.VMEM((rows, columns), jnp.float32),
                pltpu.SMEM((4, 2 * slots + UNROLL), jnp.int32),
                pltpu.SemaphoreType.DMA((columns // CHUNK,)),
            ],
        ),
        out_shape=jax.ShapeDtypeStruct((rows, width), jnp.bfloat16),
        compiler_params=pltpu.CompilerParams(vmem_limit_bytes=24 * 1024 * 1024),
        cost_estimate=pl.CostEstimate(
            flops=4 * rows * columns * width, bytes_accessed=6 * 1024 * 1024, transcendentals=0
        ),
        name="align",
    )(meta, group, queries, own, other)


def sibling(value):
    return lax.ppermute(value, "c", [(0, 1), (1, 0)])


def turned(value, distance):
    groups = lax.axis_size("x")
    return lax.ppermute(value, "x", [(i, (i + distance) % groups) for i in range(groups)])


def on_device(queries, database, pair_tiles, pair_lengths, live_pairs):
    tile, width = queries.shape
    slots = pair_tiles.shape[1]
    core = lax.axis_index("c").astype(jnp.int32)
    deep = lax.axis_index("zh").astype(jnp.int32)
    here = lax.axis_index("x").astype(jnp.int32)
    groups = lax.axis_size("x")
    places = lax.axis_size("zh")

    near = [(2 * z + c, 2 * (z ^ (1 + c)) + c) for z in range(places) for c in range(2)]
    far = [(2 * z + 1, 2 * (z ^ 3) + 1) for z in range(places)]
    first = lax.ppermute(queries, ("zh", "c"), near)
    second = lax.ppermute(queries, ("zh", "c"), far)
    panel = jnp.concatenate(
        [jnp.where(core == 0, queries, first), jnp.where(core == 0, first, second)]
    )

    other = sibling(database)
    own_meta = jnp.concatenate(
        [pair_tiles.reshape(-1), pair_lengths.reshape(-1), live_pairs, core[None], deep[None]]
    )
    own_meta = jnp.pad(own_meta, (0, 128 - own_meta.shape[0]))
    meta = jnp.concatenate([own_meta, sibling(own_meta)])

    def terms_of(rows, distance):
        group = lax.rem(here - distance + groups, groups)
        return align(meta, group[None], rows, database, other, slots)

    distances = (1, 3, 2)
    panels = [turned(panel, d) for d in distances]
    parts = [terms_of(panel, 0)]
    for distance, rows in zip(distances, panels, strict=True):
        parts.append(turned(terms_of(rows, distance), -distance))

    parts = [part.reshape(HALF, 2, tile // 2, width) for part in parts]

    def half(which):
        return sum(
            lax.dynamic_index_in_dim(part, which, 1, keepdims=False).astype(jnp.float32)
            for part in parts
        ).astype(jnp.bfloat16)

    taken = sibling(half(1 - core))
    kept = half(core)
    same = (deep >> 1) == core
    column = jnp.stack([jnp.where(same, kept, taken), jnp.where(same, taken, kept)])
    column = jnp.where((deep & 1) == 0, column, column[:, ::-1])

    pieces = lax.all_to_all(column.reshape(-1, 4, width), ("zh", "y", "zl"), 0, 0, tiled=True)
    return jnp.sum(pieces.astype(jnp.float32), axis=0).astype(jnp.bfloat16)


def solution(mesh):
    fine = Mesh(mesh.devices.reshape(4, 4, 8, 2, 2), BLK + SHARD)
    both = BLK + SHARD
    in_specs = (P(BLK, None), P(both, None), P(both, None, None), P(both, None, None), P(both))
    return jax.shard_map(
        on_device, mesh=fine, in_specs=in_specs, out_specs=P(both, None), check_vma=False
    )
```

```python
import functools

import jax
import jax.numpy as jnp
from jax import lax
from jax.experimental import pallas as pl
from jax.experimental.pallas import tpu as pltpu
from jax.sharding import Mesh
from jax.sharding import PartitionSpec as P

TILE = 128
BLK = ("x", "zh")
SHARD = ("y", "zl", "c")
HALF = 2
CHUNK = 256
UNROLL = 4


def pair_weight(scores, rows, cols, row_count, col_count):
    valid = (rows < row_count) & (cols < col_count)
    masked = jnp.where(valid, scores, -1e30)
    row_max = jnp.max(masked, axis=1, keepdims=True)
    row_lse = row_max + jnp.log(jnp.sum(jnp.exp(masked - row_max), axis=1, keepdims=True))
    col_max = jnp.max(masked, axis=0, keepdims=True)
    col_lse = col_max + jnp.log(jnp.sum(jnp.exp(masked - col_max), axis=0, keepdims=True))
    weight = jnp.where(valid, jnp.exp(scores - 0.5 * (row_lse + col_lse)), 0.0)
    return weight.astype(jnp.bfloat16)


def align_kernel(
    scale, tiles, slots, meta, group, q_ref, own_ref, other_ref, kept_ref, given_ref,
    scores, weights, listed,
):
    stride = meta.shape[0] // 2
    core = meta[4 * slots + 1]
    deep = meta[4 * slots + 2]
    width = tiles * TILE
    chunks = 2 * width // CHUNK

    weights[...] = jnp.zeros_like(weights)

    count = jnp.int32(0)
    for side in range(2):
        base = side * stride

        def look(slot, count, base=base, side=side):
            query_tile = meta[base + 2 * slot]
            near = (query_tile & 3) ^ deep
            mine = ((query_tile >> 2) == group[0]) & ((near >> 1) == core)

            @pl.when(mine)
            def _():
                listed[0, count] = near & 1
                listed[1, count] = meta[base + 2 * slot + 1] + side * tiles
                listed[2, count] = meta[base + 2 * slots + 2 * slot]
                listed[3, count] = meta[base + 2 * slots + 2 * slot + 1]

            return count + mine.astype(jnp.int32)

        count = lax.fori_loop(0, meta[base + 4 * slots], look, count)
    for extra in range(UNROLL - 1):
        for field in range(4):
            listed[field, count + extra] = 0

    across = (((1,), (1,)), ((), ()))
    query = q_ref[...]
    for index in range(chunks):
        span = slice(index * CHUNK, (index + 1) * CHUNK)
        source = own_ref if index < chunks // 2 else other_ref
        at = (index % (chunks // 2)) * CHUNK
        scores[:, span] = (
            lax.dot_general(
                query, source[at : at + CHUNK, :], across, preferred_element_type=jnp.float32
            )
            * scale
        )

    rows = lax.broadcasted_iota(jnp.int32, (TILE, TILE), 0)
    cols = lax.broadcasted_iota(jnp.int32, (TILE, TILE), 1)

    def batch(index, carry):
        made = []
        for k in range(UNROLL):
            slot = index * UNROLL + k
            at_row = pl.ds(pl.multiple_of(listed[0, slot] * TILE, TILE), TILE)
            at_col = pl.ds(pl.multiple_of(listed[1, slot] * TILE, TILE), TILE)
            weight = pair_weight(scores[at_row, at_col], rows, cols, listed[2, slot], listed[3, slot])
            made.append((at_row, at_col, weight))
        for at_row, at_col, weight in made:
            weights[at_row, at_col] += weight.astype(jnp.float32)
        return carry

    lax.fori_loop(0, (count + UNROLL - 1) // UNROLL, batch, 0)

    both = HALF * TILE
    place = lax.broadcasted_iota(jnp.int32, (both, both), 0)
    row = lax.broadcasted_iota(jnp.int32, (both, both), 1)
    goes_to = (place >> 7) ^ core
    tile = ((place >> 6) & 1) ^ (deep & 1)
    wanted = tile * TILE + ((place & 63) >> 2) * 8 + goes_to * 4 + (place & 3)
    sort = (row == wanted).astype(jnp.bfloat16)
    weight = jnp.dot(
        sort, weights[...].astype(jnp.bfloat16), preferred_element_type=jnp.float32
    ).astype(jnp.bfloat16)
    for half, ref in enumerate((kept_ref, given_ref)):
        part = weight[half * TILE : (half + 1) * TILE]
        ref[...] = (
            jnp.dot(part[:, :width], own_ref[...], preferred_element_type=jnp.float32)
            + jnp.dot(part[:, width:], other_ref[...], preferred_element_type=jnp.float32)
        ).astype(ref.dtype)


def align(meta, group, queries, own, other, slots):
    rows, width = queries.shape
    tiles = own.shape[0] // TILE
    columns = 2 * own.shape[0]
    vmem = pl.BlockSpec(memory_space=pltpu.VMEM)
    smem = pl.BlockSpec(memory_space=pltpu.SMEM)
    return pl.pallas_call(
        functools.partial(align_kernel, width ** (-0.5), tiles, slots),
        in_specs=[smem, smem, vmem, vmem, vmem],
        out_specs=[vmem, vmem],
        scratch_shapes=[
            pltpu.VMEM((rows, columns), jnp.float32),
            pltpu.VMEM((rows, columns), jnp.float32),
            pltpu.SMEM((4, 2 * slots + UNROLL), jnp.int32),
        ],
        out_shape=[jax.ShapeDtypeStruct((rows // 2, width), jnp.bfloat16)] * 2,
        compiler_params=pltpu.CompilerParams(vmem_limit_bytes=24 * 1024 * 1024),
        cost_estimate=pl.CostEstimate(
            flops=4 * rows * columns * width, bytes_accessed=6 * 1024 * 1024, transcendentals=0
        ),
        name="align",
    )(meta, group, queries, own, other)


def combine_kernel(same, *refs):
    parts, out_ref = refs[:-1], refs[-1]
    rows = parts[0].shape[0]
    count = len(parts) // 2

    def total(some):
        return sum(ref[...].astype(jnp.float32) for ref in some).astype(out_ref.dtype)

    kept_at = pl.multiple_of(jnp.where(same[0] == 1, 0, rows), rows)
    taken_at = pl.multiple_of(jnp.where(same[0] == 1, rows, 0), rows)
    out_ref[pl.ds(kept_at, rows), :] = total(parts[:count])
    out_ref[pl.ds(taken_at, rows), :] = total(parts[count:])


def combine(same, parts):
    rows, width = parts[0].shape
    vmem = pl.BlockSpec(memory_space=pltpu.VMEM)
    return pl.pallas_call(
        combine_kernel,
        in_specs=[pl.BlockSpec(memory_space=pltpu.SMEM)] + [vmem] * len(parts),
        out_specs=vmem,
        out_shape=jax.ShapeDtypeStruct((2 * rows, width), jnp.bfloat16),
        compiler_params=pltpu.CompilerParams(vmem_limit_bytes=24 * 1024 * 1024),
        cost_estimate=pl.CostEstimate(
            flops=len(parts) * rows * width, bytes_accessed=0, transcendentals=0
        ),
        name="combine",
    )(same, *parts)


def sibling(value):
    return lax.ppermute(value, "c", [(0, 1), (1, 0)])


def turned(value, distance, crossed):
    groups = lax.axis_size("x")
    route = [
        (2 * i + c, 2 * ((i + distance) % groups) + (c ^ crossed))
        for i in range(groups)
        for c in range(2)
    ]
    return lax.ppermute(value, ("x", "c"), route)


def on_device(queries, database, pair_tiles, pair_lengths, live_pairs):
    tile, width = queries.shape
    slots = pair_tiles.shape[1]
    core = lax.axis_index("c").astype(jnp.int32)
    deep = lax.axis_index("zh").astype(jnp.int32)
    here = lax.axis_index("x").astype(jnp.int32)
    groups = lax.axis_size("x")
    places = lax.axis_size("zh")

    near = [(2 * z + c, 2 * (z ^ (1 + c)) + c) for z in range(places) for c in range(2)]
    far = [(2 * z + 1, 2 * (z ^ 3) + 1) for z in range(places)]
    first = lax.ppermute(queries, ("zh", "c"), near)
    second = lax.ppermute(queries, ("zh", "c"), far)
    panel = jnp.concatenate(
        [jnp.where(core == 0, queries, first), jnp.where(core == 0, first, second)]
    )

    own_meta = jnp.concatenate(
        [pair_tiles.reshape(-1), pair_lengths.reshape(-1), live_pairs, core[None], deep[None]]
    )
    own_meta = jnp.pad(own_meta, (0, 128 - own_meta.shape[0]))
    panel, database, own_meta = lax.optimization_barrier((panel, database, own_meta))
    other = sibling(database)
    meta = jnp.concatenate([own_meta, sibling(own_meta)])

    def terms_of(rows, distance):
        group = lax.rem(here - distance + groups, groups)
        return align(meta, group[None], rows, database, other, slots)

    distances = (1, 3, 2)
    panels = [turned(panel, d, 0) for d in distances]
    kept, given = terms_of(panel, 0)
    kept, panels[0] = lax.optimization_barrier((kept, panels[0]))
    own_parts, other_parts = [kept], [sibling(given)]
    for distance, rows in zip(distances, panels, strict=True):
        kept, given = terms_of(rows, distance)
        own_parts.append(turned(kept, -distance, 0))
        other_parts.append(turned(given, -distance, 1))

    same = ((deep >> 1) == core).astype(jnp.int32)
    column = combine(same[None], own_parts + other_parts)
    pieces = lax.all_to_all(column.reshape(-1, 4, width), ("zh", "y", "zl"), 0, 0, tiled=True)
    return jnp.sum(pieces.astype(jnp.float32), axis=0).astype(jnp.bfloat16)


def solution(mesh):
    fine = Mesh(mesh.devices.reshape(4, 4, 8, 2, 2), BLK + SHARD)
    both = BLK + SHARD
    in_specs = (P(BLK, None), P(both, None), P(both, None, None), P(both, None, None), P(both))
    return jax.shard_map(
        on_device, mesh=fine, in_specs=in_specs, out_specs=P(both, None), check_vma=False
    )
```

```python
import functools
import math

import jax
import jax.numpy as jnp
from jax import lax
from jax.experimental import pallas as pl
from jax.experimental.pallas import tpu as pltpu
from jax.sharding import Mesh
from jax.sharding import PartitionSpec as P

TILE = 128
BLK = ("x", "zh")
SHARD = ("yq", "yp", "zl", "c")
HALF = 2
CHUNK = 256
UNROLL = 4
LIST = 64


def pair_weight(scores, rows, cols, row_count, col_count):
    valid = (rows < row_count) & (cols < col_count)
    masked = jnp.where(valid, scores, -1e30)
    row_max = jnp.max(masked, axis=1, keepdims=True)
    row_lse = row_max + jnp.log(jnp.sum(jnp.exp(masked - row_max), axis=1, keepdims=True))
    col_max = jnp.max(masked, axis=0, keepdims=True)
    col_lse = col_max + jnp.log(jnp.sum(jnp.exp(masked - col_max), axis=0, keepdims=True))
    weight = jnp.where(valid, jnp.exp(scores - 0.5 * (row_lse + col_lse)), 0.0)
    return weight.astype(jnp.bfloat16)


def plan_kernel(tiles, slots, meta, lists):
    stride = meta.shape[0] // 2
    core, deep, here = (meta[4 * slots + 1 + k] for k in range(3))
    groups = lists.shape[0] // LIST
    for group in range(groups):
        lists[group * LIST] = 0
    for side in range(2):
        base = side * stride

        def look(slot, carry, base=base, side=side):
            query_tile = meta[base + 2 * slot]
            near = (query_tile & 3) ^ deep

            @pl.when((near >> 1) == core)
            def _():
                at = (query_tile >> 2) * LIST
                count = lists[at] + 1
                lists[at] = count
                lists[at + count] = (
                    (near & 1)
                    + 2 * (meta[base + 2 * slot + 1] + side * tiles)
                    + 256 * meta[base + 2 * slots + 2 * slot]
                    + 65536 * meta[base + 2 * slots + 2 * slot + 1]
                )

            return carry

        lax.fori_loop(0, meta[base + 4 * slots], look, 0)
    for group in range(groups):
        count = lists[group * LIST]
        for extra in range(1, UNROLL):
            lists[group * LIST + count + extra] = 0
    lists[groups * LIST - 3] = core
    lists[groups * LIST - 2] = deep
    lists[groups * LIST - 1] = here


def plan(meta, tiles, slots, groups):
    smem = pl.BlockSpec(memory_space=pltpu.SMEM)
    return pl.pallas_call(
        functools.partial(plan_kernel, tiles, slots),
        in_specs=[smem],
        out_specs=smem,
        out_shape=jax.ShapeDtypeStruct((groups * LIST,), jnp.int32),
        name="plan",
    )(meta)


def align_kernel(scale, distance, lists, q_ref, own_ref, other_ref, *refs):
    out_ref, scores, weights = refs[-3:]
    groups = lists.shape[0] // LIST
    core, deep, here = (lists[groups * LIST - 3 + k] for k in range(3))
    group = (here - distance) & (groups - 1)
    width = own_ref.shape[0]
    weights[...] = jnp.zeros_like(weights)

    across = (((1,), (1,)), ((), ()))
    query = q_ref[...]
    for side, ref in enumerate((own_ref, other_ref)):
        for first in range(0, width, CHUNK):
            scores[:, side * width + first : side * width + first + CHUNK] = (
                lax.dot_general(
                    query, ref[first : first + CHUNK, :], across, preferred_element_type=jnp.float32
                )
                * scale
            )

    rows = lax.broadcasted_iota(jnp.int32, (TILE, TILE), 0)
    cols = lax.broadcasted_iota(jnp.int32, (TILE, TILE), 1)
    start = group * LIST

    def batch(index, carry):
        made = []
        for k in range(UNROLL):
            slot = lists[start + 1 + index * UNROLL + k]
            at_row = pl.ds(pl.multiple_of((slot & 1) * TILE, TILE), TILE)
            at_col = pl.ds(pl.multiple_of(((slot >> 1) & 127) * TILE, TILE), TILE)
            weight = pair_weight(
                scores[at_row, at_col], rows, cols, (slot >> 8) & 255, slot >> 16
            )
            made.append((at_row, at_col, weight))
        for at_row, at_col, weight in made:
            weights[at_row, at_col] += weight.astype(jnp.float32)
        return carry

    lax.fori_loop(0, (lists[start] + UNROLL - 1) // UNROLL, batch, 0)

    both = HALF * TILE
    place = lax.broadcasted_iota(jnp.int32, (both, both), 0)
    row = lax.broadcasted_iota(jnp.int32, (both, both), 1)
    tile = ((place >> 4) & 1) ^ (deep & 1)
    wanted = tile * TILE + ((place >> 2) & 3) * 32 + (place >> 5) * 4 + (place & 3)
    sort = (row == wanted).astype(jnp.bfloat16)
    weight = jnp.dot(
        sort, weights[...].astype(jnp.bfloat16), preferred_element_type=jnp.float32
    ).astype(jnp.bfloat16)
    out_ref[pl.ds(pl.multiple_of(group * both, both), both), :] = (
        jnp.dot(weight[:, :width], own_ref[...], preferred_element_type=jnp.float32)
        + jnp.dot(weight[:, width:], other_ref[...], preferred_element_type=jnp.float32)
    ).astype(out_ref.dtype)


def align(lists, distance, queries, own, other, sofar):
    rows, width = queries.shape
    groups = lists.shape[0] // LIST
    columns = 2 * own.shape[0]
    vmem = pl.BlockSpec(memory_space=pltpu.VMEM)
    return pl.pallas_call(
        functools.partial(align_kernel, width ** (-0.5), distance),
        in_specs=[pl.BlockSpec(memory_space=pltpu.SMEM)] + [vmem] * (3 + len(sofar)),
        out_specs=vmem,
        scratch_shapes=[
            pltpu.VMEM((rows, columns), jnp.float32),
            pltpu.VMEM((rows, columns), jnp.float32),
        ],
        out_shape=jax.ShapeDtypeStruct((groups * rows, width), jnp.bfloat16),
        input_output_aliases={4: 0} if sofar else {},
        compiler_params=pltpu.CompilerParams(vmem_limit_bytes=24 * 1024 * 1024),
        cost_estimate=pl.CostEstimate(
            flops=4 * rows * columns * width, bytes_accessed=6 * 1024 * 1024, transcendentals=0
        ),
        name="align",
    )(lists, queries, own, other, *sofar)


def combine_kernel(cores, lists, parts_ref, out_ref):
    peers, rows, _ = parts_ref.shape
    deep = lists[lists.shape[0] - 2]
    for core in range(cores):
        total = sum(
            parts_ref[peer].astype(jnp.float32) for peer in range(core, peers, cores)
        ).astype(out_ref.dtype)
        out_ref[pl.ds(pl.multiple_of((core ^ (deep >> 1)) * rows, rows), rows), :] = total


def combine(lists, parts, cores):
    peers, rows, width = parts.shape
    vmem = pl.BlockSpec(memory_space=pltpu.VMEM)
    return pl.pallas_call(
        functools.partial(combine_kernel, cores),
        in_specs=[pl.BlockSpec(memory_space=pltpu.SMEM), vmem],
        out_specs=vmem,
        out_shape=jax.ShapeDtypeStruct((cores * rows, width), jnp.bfloat16),
        compiler_params=pltpu.CompilerParams(vmem_limit_bytes=24 * 1024 * 1024),
        cost_estimate=pl.CostEstimate(
            flops=peers * rows * width, bytes_accessed=0, transcendentals=0
        ),
        name="combine",
    )(lists, parts)


def sibling(value):
    return lax.ppermute(value, "c", [(0, 1), (1, 0)])


def turned(value, distance):
    groups = lax.axis_size("x")
    return lax.ppermute(value, "x", [(i, (i + distance) % groups) for i in range(groups)])


def on_device(queries, database, pair_tiles, pair_lengths, live_pairs):
    tile, width = queries.shape
    slots = pair_tiles.shape[1]
    core = lax.axis_index("c").astype(jnp.int32)
    deep = lax.axis_index("zh").astype(jnp.int32)
    here = lax.axis_index("x").astype(jnp.int32)
    groups = lax.axis_size("x")
    places = lax.axis_size("zh")

    near = [(2 * z + c, 2 * (z ^ (1 + c)) + c) for z in range(places) for c in range(2)]
    far = [(2 * z + 1, 2 * (z ^ 3) + 1) for z in range(places)]
    first = lax.ppermute(queries, ("zh", "c"), near)
    second = lax.ppermute(queries, ("zh", "c"), far)
    panel = jnp.concatenate(
        [jnp.where(core == 0, queries, first), jnp.where(core == 0, first, second)]
    )

    own_meta = jnp.concatenate(
        [pair_tiles.reshape(-1), pair_lengths.reshape(-1), live_pairs]
        + [axis[None] for axis in (core, deep, here)]
    )
    own_meta = jnp.pad(own_meta, (0, 128 - own_meta.shape[0]))
    lists = plan(
        jnp.concatenate([own_meta, sibling(own_meta)]), database.shape[0] // tile, slots, groups
    )
    panel, database = lax.optimization_barrier((panel, database))
    other = sibling(database)

    distances = (1, 3, 2)
    panels = [turned(panel, d) for d in distances]
    terms = align(lists, 0, panel, database, other, [])
    for distance, rows in zip(distances, panels, strict=True):
        terms = align(lists, distance, rows, database, other, [terms])

    near_axes = ("x", "yp", "zl", "c")
    peers = math.prod(lax.axis_size(axis) for axis in near_axes)
    parts = lax.all_to_all(terms.reshape(peers, -1, width), near_axes, 0, 0, tiled=True)
    column = combine(lists, parts, lax.axis_size("c"))
    pieces = lax.all_to_all(column.reshape(-1, 4, width), ("zh", "yq"), 0, 0, tiled=True)
    return jnp.sum(pieces.astype(jnp.float32), axis=0).astype(jnp.bfloat16)


def solution(mesh):
    fine = Mesh(mesh.devices.reshape(4, 4, 4, 2, 2, 2), BLK + SHARD)
    both = BLK + SHARD
    in_specs = (P(BLK, None), P(both, None), P(both, None, None), P(both, None, None), P(both))
    return jax.shard_map(
        on_device, mesh=fine, in_specs=in_specs, out_specs=P(both, None), check_vma=False
    )
```

```python
import functools
import math

import jax
import jax.numpy as jnp
from jax import lax
from jax.experimental import pallas as pl
from jax.experimental.pallas import tpu as pltpu
from jax.sharding import Mesh
from jax.sharding import PartitionSpec as P

TILE = 128
BLK = ("x", "zh")
SHARD = ("yq", "yp", "zl", "c")
QUARTERS = 4
HALF = 2
CHUNK = 256
UNROLL = 4


def pair_weight(scores, rows, cols, row_count, col_count):
    valid = (rows < row_count) & (cols < col_count)
    masked = jnp.where(valid, scores, -1e30)
    row_max = jnp.max(masked, axis=1, keepdims=True)
    row_lse = row_max + jnp.log(jnp.sum(jnp.exp(masked - row_max), axis=1, keepdims=True))
    col_max = jnp.max(masked, axis=0, keepdims=True)
    col_lse = col_max + jnp.log(jnp.sum(jnp.exp(masked - col_max), axis=0, keepdims=True))
    weight = jnp.where(valid, jnp.exp(scores - 0.5 * (row_lse + col_lse)), 0.0)
    return weight.astype(jnp.bfloat16)


def spread_kernel(place, own_ref, first_ref, second_ref, out_ref):
    rows = own_ref.shape[0]
    near = place[0] == 0
    tiles = jnp.where(near, own_ref[...], first_ref[...]), jnp.where(near, first_ref[...], second_ref[...])
    for peer in range(out_ref.shape[0]):
        for index, tile in enumerate(tiles):
            out_ref[peer, index * rows : (index + 1) * rows, :] = tile


def spread(place, own, first, second, peers):
    rows, width = own.shape
    vmem = pl.BlockSpec(memory_space=pltpu.VMEM)
    return pl.pallas_call(
        spread_kernel,
        in_specs=[pl.BlockSpec(memory_space=pltpu.SMEM)] + [vmem] * 3,
        out_specs=vmem,
        out_shape=jax.ShapeDtypeStruct((peers, HALF * rows, width), jnp.bfloat16),
        name="spread",
    )(place, own, first, second)


def plan_kernel(tiles, slots, place, meta, lists):
    stride = meta.shape[0] // 2
    core, deep = place[0], place[1]
    lists[0] = 0
    for side in range(2):
        base = side * stride

        def look(slot, carry, base=base, side=side):
            query_tile = meta[base + 2 * slot]
            near = (query_tile & 3) ^ deep

            @pl.when((near >> 1) == core)
            def _():
                count = lists[0] + 1
                lists[0] = count
                lists[count] = (
                    (near & 1)
                    + 2 * (query_tile >> 2)
                    + 16 * (meta[base + 2 * slot + 1] + side * tiles)
                    + 256 * meta[base + 2 * slots + 2 * slot]
                    + 65536 * meta[base + 2 * slots + 2 * slot + 1]
                )

            return carry

        lax.fori_loop(0, meta[base + 4 * slots], look, 0)
    for extra in range(1, UNROLL):
        lists[lists[0] + extra] = 0


def plan(place, meta, tiles, slots):
    smem = pl.BlockSpec(memory_space=pltpu.SMEM)
    return pl.pallas_call(
        functools.partial(plan_kernel, tiles, slots),
        in_specs=[smem, smem],
        out_specs=smem,
        out_shape=jax.ShapeDtypeStruct((2 * slots + 1 + UNROLL,), jnp.int32),
        name="plan",
    )(place, meta)


def align_kernel(scale, place, lists, q_ref, own_ref, other_ref, out_ref, scores, weights):
    deep = place[1]
    total, _ = q_ref.shape
    width = own_ref.shape[0]
    group = HALF * TILE
    piece = TILE // QUARTERS

    across = (((1,), (1,)), ((), ()))
    for first in range(0, total, group):
        weights[first : first + group, :] = jnp.zeros((group, 2 * width), weights.dtype)
        query = q_ref[first : first + group, :]
        for side, ref in enumerate((own_ref, other_ref)):
            for at in range(0, width, CHUNK):
                scores[first : first + group, side * width + at : side * width + at + CHUNK] = (
                    lax.dot_general(
                        query, ref[at : at + CHUNK, :], across, preferred_element_type=jnp.float32
                    )
                    * scale
                )

    place_in_tile = lax.broadcasted_iota(jnp.int32, (TILE, TILE), 0)
    rows = ((place_in_tile >> 3) & 3) * 32 + (place_in_tile >> 5) * 8 + (place_in_tile & 7)
    cols = lax.broadcasted_iota(jnp.int32, (TILE, TILE), 1)

    def batch(index, carry):
        made = []
        for k in range(UNROLL):
            slot = lists[1 + index * UNROLL + k]
            first = ((slot >> 1) & 7) * group + (slot & 1) * piece
            at_rows = [
                pl.ds(pl.multiple_of(first + quarter * HALF * piece, piece), piece)
                for quarter in range(QUARTERS)
            ]
            at_col = pl.ds(pl.multiple_of(((slot >> 4) & 15) * TILE, TILE), TILE)
            score = jnp.concatenate([scores[at_row, at_col] for at_row in at_rows])
            weight = pair_weight(score, rows, cols, (slot >> 8) & 255, slot >> 16)
            made.append((at_rows, at_col, weight))
        for at_rows, at_col, weight in made:
            for quarter, at_row in enumerate(at_rows):
                weights[at_row, at_col] += weight[
                    quarter * piece : (quarter + 1) * piece
                ].astype(jnp.float32)
        return carry

    lax.fori_loop(0, (lists[0] + UNROLL - 1) // UNROLL, batch, 0)

    to = lax.broadcasted_iota(jnp.int32, (group, group), 0)
    row = lax.broadcasted_iota(jnp.int32, (group, group), 1)
    tile = ((to >> 4) & 1) ^ (deep & 1)
    wanted = (to >> 6) * 64 + tile * 32 + ((to >> 2) & 3) * 8 + ((to >> 5) & 1) * 4 + (to & 3)
    sort = (row == wanted).astype(jnp.bfloat16)
    for first in range(0, total, group):
        weight = jnp.dot(
            sort,
            weights[first : first + group, :].astype(jnp.bfloat16),
            preferred_element_type=jnp.float32,
        ).astype(jnp.bfloat16)
        out_ref[first : first + group, :] = (
            jnp.dot(weight[:, :width], own_ref[...], preferred_element_type=jnp.float32)
            + jnp.dot(weight[:, width:], other_ref[...], preferred_element_type=jnp.float32)
        ).astype(out_ref.dtype)


def align(place, lists, queries, own, other):
    rows, width = queries.shape
    columns = 2 * own.shape[0]
    smem = pl.BlockSpec(memory_space=pltpu.SMEM)
    vmem = pl.BlockSpec(memory_space=pltpu.VMEM)
    return pl.pallas_call(
        functools.partial(align_kernel, width ** (-0.5)),
        in_specs=[smem, smem, vmem, vmem, vmem],
        out_specs=vmem,
        scratch_shapes=[
            pltpu.VMEM((rows, columns), jnp.float32),
            pltpu.VMEM((rows, columns), jnp.float32),
        ],
        out_shape=jax.ShapeDtypeStruct((rows, width), jnp.bfloat16),
        compiler_params=pltpu.CompilerParams(vmem_limit_bytes=24 * 1024 * 1024),
        cost_estimate=pl.CostEstimate(
            flops=4 * rows * columns * width, bytes_accessed=0, transcendentals=0
        ),
        name="align",
    )(place, lists, queries, own, other)


def combine_kernel(cores, place, parts_ref, out_ref):
    peers, rows, _ = parts_ref.shape
    deep = place[1]
    for core in range(cores):
        total = sum(
            parts_ref[peer].astype(jnp.float32) for peer in range(core, peers, cores)
        ).astype(out_ref.dtype)
        out_ref[pl.ds(pl.multiple_of((core ^ (deep >> 1)) * rows, rows), rows), :] = total


def combine(place, parts, cores):
    peers, rows, width = parts.shape
    vmem = pl.BlockSpec(memory_space=pltpu.VMEM)
    return pl.pallas_call(
        functools.partial(combine_kernel, cores),
        in_specs=[pl.BlockSpec(memory_space=pltpu.SMEM), vmem],
        out_specs=vmem,
        out_shape=jax.ShapeDtypeStruct((cores * rows, width), jnp.bfloat16),
        compiler_params=pltpu.CompilerParams(vmem_limit_bytes=24 * 1024 * 1024),
        cost_estimate=pl.CostEstimate(
            flops=peers * rows * width, bytes_accessed=0, transcendentals=0
        ),
        name="combine",
    )(place, parts)


def sibling(value):
    return lax.ppermute(value, "c", [(0, 1), (1, 0)])


def on_device(queries, database, pair_tiles, pair_lengths, live_pairs):
    tile, width = queries.shape
    slots = pair_tiles.shape[1]
    core = lax.axis_index("c").astype(jnp.int32)
    deep = lax.axis_index("zh").astype(jnp.int32)
    place = jnp.stack([core, deep])
    places = lax.axis_size("zh")

    quarter = queries.reshape(lax.axis_size("yq"), 2, 2, 8, width)
    quarter = lax.dynamic_index_in_dim(quarter, lax.axis_index("yp"), 1, keepdims=False)
    quarter = lax.dynamic_index_in_dim(quarter, lax.axis_index("zl"), 1, keepdims=False)
    quarter = quarter.reshape(tile // QUARTERS, width)
    near = [(2 * z + c, 2 * (z ^ (1 + c)) + c) for z in range(places) for c in range(2)]
    far = [(2 * z + 1, 2 * (z ^ 3) + 1) for z in range(places)]
    first = lax.ppermute(quarter, ("zh", "c"), near)
    second = lax.ppermute(quarter, ("zh", "c"), far)

    own_meta = jnp.concatenate([pair_tiles.reshape(-1), pair_lengths.reshape(-1), live_pairs])
    own_meta = jnp.pad(own_meta, (0, 128 - own_meta.shape[0]))
    meta = jnp.concatenate([own_meta, sibling(own_meta)])
    lists = plan(place, meta, database.shape[0] // tile, slots)

    around = ("x", "yp", "zl")
    peers = math.prod(lax.axis_size(axis) for axis in around)
    panel = spread(place, quarter, first, second, peers)
    panel, database = lax.optimization_barrier((panel, database))
    other = sibling(database)
    panels = lax.all_to_all(panel, around, 0, 0, tiled=True).reshape(-1, width)

    terms = align(place, lists, panels, database, other)

    around = ("x", "yp", "zl", "c")
    peers = math.prod(lax.axis_size(axis) for axis in around)
    parts = lax.all_to_all(terms.reshape(peers, -1, width), around, 0, 0, tiled=True)
    column = combine(place, parts, lax.axis_size("c"))
    pieces = lax.all_to_all(column.reshape(-1, 4, width), ("zh", "yq"), 0, 0, tiled=True)
    return jnp.sum(pieces.astype(jnp.float32), axis=0).astype(jnp.bfloat16)


def solution(mesh):
    fine = Mesh(mesh.devices.reshape(4, 4, 4, 2, 2, 2), BLK + SHARD)
    both = BLK + SHARD
    in_specs = (P(BLK, None), P(both, None), P(both, None, None), P(both, None, None), P(both))
    return jax.shard_map(
        on_device, mesh=fine, in_specs=in_specs, out_specs=P(both, None), check_vma=False
    )
```

```python
import functools
import math

import jax
import jax.numpy as jnp
from jax import lax
from jax.experimental import pallas as pl
from jax.experimental.pallas import tpu as pltpu
from jax.sharding import Mesh
from jax.sharding import PartitionSpec as P

TILE = 128
BLK = ("x", "zh")
SHARD = ("yq", "yp", "zl", "c")
QUARTERS = 4
HALF = 2
CHUNK = 256
UNROLL = 4


def pair_weight(scores, rows, cols, row_count, col_count):
    valid = (rows < row_count) & (cols < col_count)
    masked = jnp.where(valid, scores, -1e30)
    row_max = jnp.max(masked, axis=1, keepdims=True)
    row_lse = row_max + jnp.log(jnp.sum(jnp.exp(masked - row_max), axis=1, keepdims=True))
    col_max = jnp.max(masked, axis=0, keepdims=True)
    col_lse = col_max + jnp.log(jnp.sum(jnp.exp(masked - col_max), axis=0, keepdims=True))
    weight = jnp.where(valid, jnp.exp(scores - 0.5 * (row_lse + col_lse)), 0.0)
    return weight.astype(jnp.bfloat16)


def spread_kernel(place, own_ref, first_ref, second_ref, out_ref, held, sent):
    near, odd = place[0] == 0, place[1] & 1
    both = jnp.concatenate(
        [
            jnp.where(near, own_ref[...], first_ref[...]),
            jnp.where(near, first_ref[...], second_ref[...]),
        ]
    )
    count = both.shape[0]
    to = lax.broadcasted_iota(jnp.int32, (count, count), 0)
    row = lax.broadcasted_iota(jnp.int32, (count, count), 1)
    wanted = (((to >> 4) & 1) ^ odd) * 32 + ((to >> 2) & 3) * 8 + (to >> 5) * 4 + (to & 3)
    both = jnp.dot(
        (row == wanted).astype(both.dtype), both, preferred_element_type=jnp.float32
    ).astype(both.dtype)
    held[...] = both
    copies = [
        pltpu.make_async_copy(held, out_ref.at[peer], sent.at[peer])
        for peer in range(out_ref.shape[0])
    ]
    for copy in copies:
        copy.start()
    for copy in copies:
        copy.wait()


def spread(place, own, first, second, peers):
    rows, width = own.shape
    vmem = pl.BlockSpec(memory_space=pltpu.VMEM)
    return pl.pallas_call(
        spread_kernel,
        in_specs=[pl.BlockSpec(memory_space=pltpu.SMEM)] + [vmem] * 3,
        out_specs=pl.BlockSpec(memory_space=pl.ANY),
        scratch_shapes=[
            pltpu.VMEM((HALF * rows, width), jnp.bfloat16),
            pltpu.SemaphoreType.DMA((peers,)),
        ],
        out_shape=jax.ShapeDtypeStruct((peers, HALF * rows, width), jnp.bfloat16),
        compiler_params=pltpu.CompilerParams(vmem_limit_bytes=8 * 1024 * 1024),
        name="spread",
    )(place, own, first, second)


def plan_kernel(tiles, slots, place, meta, lists):
    stride = meta.shape[0] // 2
    core, deep = place[0], place[1]
    lists[0] = 0
    for side in range(2):
        base = side * stride

        def look(slot, carry, base=base, side=side):
            query_tile = meta[base + 2 * slot]
            near = (query_tile & 3) ^ deep

            @pl.when((near >> 1) == core)
            def _():
                count = lists[0] + 1
                lists[0] = count
                lists[count] = (
                    (query_tile & 1)
                    + 2 * (query_tile >> 2)
                    + 16 * (meta[base + 2 * slot + 1] + side * tiles)
                    + 256 * meta[base + 2 * slots + 2 * slot]
                    + 65536 * meta[base + 2 * slots + 2 * slot + 1]
                )

            return carry

        lax.fori_loop(0, meta[base + 4 * slots], look, 0)
    for extra in range(1, UNROLL):
        lists[lists[0] + extra] = 0


def plan(place, meta, tiles, slots):
    smem = pl.BlockSpec(memory_space=pltpu.SMEM)
    return pl.pallas_call(
        functools.partial(plan_kernel, tiles, slots),
        in_specs=[smem, smem],
        out_specs=smem,
        out_shape=jax.ShapeDtypeStruct((2 * slots + 1 + UNROLL,), jnp.int32),
        compiler_params=pltpu.CompilerParams(vmem_limit_bytes=1024 * 1024),
        name="plan",
    )(place, meta)


def align_kernel(scale, lists, q_ref, own_ref, other_ref, out_ref, scores, weights):
    total, _ = q_ref.shape
    width = own_ref.shape[0]
    group = HALF * TILE
    pieces = 2 * QUARTERS
    piece = TILE // pieces

    across = (((1,), (1,)), ((), ()))
    for first in range(0, total, group):
        weights[first : first + group, :] = jnp.zeros((group, 2 * width), weights.dtype)
        query = q_ref[first : first + group, :]
        for side, ref in enumerate((own_ref, other_ref)):
            for at in range(0, width, CHUNK):
                scores[first : first + group, side * width + at : side * width + at + CHUNK] = (
                    lax.dot_general(
                        query, ref[at : at + CHUNK, :], across, preferred_element_type=jnp.float32
                    )
                    * scale
                )

    place_in_tile = lax.broadcasted_iota(jnp.int32, (TILE, TILE), 0)
    rows = (
        ((place_in_tile >> 2) & 3) * 32
        + (place_in_tile >> 5) * 8
        + ((place_in_tile >> 4) & 1) * 4
        + (place_in_tile & 3)
    )
    cols = lax.broadcasted_iota(jnp.int32, (TILE, TILE), 1)

    def batch(index, carry):
        made = []
        for k in range(UNROLL):
            slot = lists[1 + index * UNROLL + k]
            first = ((slot >> 1) & 7) * group + (slot & 1) * piece
            at_rows = [
                pl.ds(pl.multiple_of(first + step * HALF * piece, piece), piece)
                for step in range(pieces)
            ]
            at_col = pl.ds(pl.multiple_of(((slot >> 4) & 15) * TILE, TILE), TILE)
            score = jnp.concatenate([scores[at_row, at_col] for at_row in at_rows])
            weight = pair_weight(score, rows, cols, (slot >> 8) & 255, slot >> 16)
            made.append((at_rows, at_col, weight))
        for at_rows, at_col, weight in made:
            for step, at_row in enumerate(at_rows):
                weights[at_row, at_col] += weight[step * piece : (step + 1) * piece].astype(
                    weights.dtype
                )
        return carry

    lax.fori_loop(0, (lists[0] + UNROLL - 1) // UNROLL, batch, 0)

    for first in range(0, total, group):
        weight = weights[first : first + group, :].astype(jnp.bfloat16)
        out_ref[first : first + group, :] = (
            jnp.dot(weight[:, :width], own_ref[...], preferred_element_type=jnp.float32)
            + jnp.dot(weight[:, width:], other_ref[...], preferred_element_type=jnp.float32)
        ).astype(out_ref.dtype)


def align(lists, queries, own, other):
    rows, width = queries.shape
    columns = 2 * own.shape[0]
    smem = pl.BlockSpec(memory_space=pltpu.SMEM)
    vmem = pl.BlockSpec(memory_space=pltpu.VMEM)
    return pl.pallas_call(
        functools.partial(align_kernel, width ** (-0.5)),
        in_specs=[smem, vmem, vmem, vmem],
        out_specs=vmem,
        scratch_shapes=[
            pltpu.VMEM((rows, columns), jnp.float32),
            pltpu.VMEM((rows, columns), jnp.bfloat16),
        ],
        out_shape=jax.ShapeDtypeStruct((rows, width), jnp.bfloat16),
        compiler_params=pltpu.CompilerParams(vmem_limit_bytes=24 * 1024 * 1024),
        cost_estimate=pl.CostEstimate(
            flops=4 * rows * columns * width, bytes_accessed=0, transcendentals=0
        ),
        name="align",
    )(lists, queries, own, other)


def combine_kernel(cores, place, parts_ref, out_ref):
    peers, rows, _ = parts_ref.shape
    deep = place[1]
    for core in range(cores):
        total = sum(
            parts_ref[peer].astype(jnp.float32) for peer in range(core, peers, cores)
        ).astype(out_ref.dtype)
        out_ref[pl.ds(pl.multiple_of((core ^ (deep >> 1)) * rows, rows), rows), :] = total


def combine(place, parts, cores):
    peers, rows, width = parts.shape
    vmem = pl.BlockSpec(memory_space=pltpu.VMEM)
    return pl.pallas_call(
        functools.partial(combine_kernel, cores),
        in_specs=[pl.BlockSpec(memory_space=pltpu.SMEM), vmem],
        out_specs=vmem,
        out_shape=jax.ShapeDtypeStruct((cores * rows, width), jnp.bfloat16),
        compiler_params=pltpu.CompilerParams(vmem_limit_bytes=24 * 1024 * 1024),
        cost_estimate=pl.CostEstimate(
            flops=peers * rows * width, bytes_accessed=0, transcendentals=0
        ),
        name="combine",
    )(place, parts)


def sibling(value):
    return lax.ppermute(value, "c", [(0, 1), (1, 0)])


def on_device(queries, database, pair_tiles, pair_lengths, live_pairs):
    tile, width = queries.shape
    slots = pair_tiles.shape[1]
    core = lax.axis_index("c").astype(jnp.int32)
    deep = lax.axis_index("zh").astype(jnp.int32)
    place = jnp.stack([core, deep])
    places = lax.axis_size("zh")

    quarter = queries.reshape(lax.axis_size("yq"), 2, 2, 8, width)
    quarter = lax.dynamic_index_in_dim(quarter, lax.axis_index("yp"), 1, keepdims=False)
    quarter = lax.dynamic_index_in_dim(quarter, lax.axis_index("zl"), 1, keepdims=False)
    quarter = quarter.reshape(tile // QUARTERS, width)
    near = [(2 * z + c, 2 * (z ^ (1 + c)) + c) for z in range(places) for c in range(2)]
    far = [(2 * z + 1, 2 * (z ^ 3) + 1) for z in range(places)]
    quarter, database = lax.optimization_barrier((quarter, database))
    first = lax.ppermute(quarter, ("zh", "c"), near)
    second = lax.ppermute(quarter, ("zh", "c"), far)

    own_meta = jnp.concatenate([pair_tiles.reshape(-1), pair_lengths.reshape(-1), live_pairs])
    own_meta = jnp.pad(own_meta, (0, 128 - own_meta.shape[0]))
    meta = jnp.concatenate([own_meta, sibling(own_meta)])
    lists = plan(place, meta, database.shape[0] // tile, slots)
    other = sibling(database)

    around = ("x", "yp", "zl")
    peers = math.prod(lax.axis_size(axis) for axis in around)
    panel = spread(place, quarter, first, second, peers)
    panel, other = lax.optimization_barrier((panel, other))
    panels = lax.all_to_all(panel, around, 0, 0, tiled=True).reshape(-1, width)

    terms = align(lists, panels, database, other)

    around = ("x", "yp", "zl", "c")
    peers = math.prod(lax.axis_size(axis) for axis in around)
    parts = lax.all_to_all(terms.reshape(peers, -1, width), around, 0, 0, tiled=True)
    column = combine(place, parts, lax.axis_size("c"))
    pieces = lax.all_to_all(column.reshape(-1, 4, width), ("zh", "yq"), 0, 0, tiled=True)
    return jnp.sum(pieces.astype(jnp.float32), axis=0).astype(jnp.bfloat16)


def solution(mesh):
    fine = Mesh(mesh.devices.reshape(4, 4, 4, 2, 2, 2), BLK + SHARD)
    both = BLK + SHARD
    in_specs = (P(BLK, None), P(both, None), P(both, None, None), P(both, None, None), P(both))
    return jax.shard_map(
        on_device, mesh=fine, in_specs=in_specs, out_specs=P(both, None), check_vma=False
    )
```

```python
import functools
import math

import jax
import jax.numpy as jnp
from jax import lax
from jax.experimental import pallas as pl
from jax.experimental.pallas import tpu as pltpu
from jax.sharding import Mesh
from jax.sharding import PartitionSpec as P

TILE = 128
BLK = ("x", "zh")
SHARD = ("yq", "yp", "zl", "c")
QUARTERS = 4
HALF = 2
CHUNK = 256
UNROLL = 4


def pair_weight(scores, rows, cols, row_count, col_count):
    valid = (rows < row_count) & (cols < col_count)
    masked = jnp.where(valid, scores, -1e30)
    row_max = jnp.max(masked, axis=1, keepdims=True)
    row_lse = row_max + jnp.log(jnp.sum(jnp.exp(masked - row_max), axis=1, keepdims=True))
    col_max = jnp.max(masked, axis=0, keepdims=True)
    col_lse = col_max + jnp.log(jnp.sum(jnp.exp(masked - col_max), axis=0, keepdims=True))
    weight = jnp.where(valid, jnp.exp(scores - 0.5 * (row_lse + col_lse)), 0.0)
    return weight.astype(jnp.bfloat16)


def spread_kernel(place, own_ref, first_ref, second_ref, out_ref, held, sent):
    near, odd = place[0] == 0, place[1] & 1
    both = jnp.concatenate(
        [
            jnp.where(near, own_ref[...], first_ref[...]),
            jnp.where(near, first_ref[...], second_ref[...]),
        ]
    )
    count = both.shape[0]
    to = lax.broadcasted_iota(jnp.int32, (count, count), 0)
    row = lax.broadcasted_iota(jnp.int32, (count, count), 1)
    wanted = (((to >> 4) & 1) ^ odd) * 32 + ((to >> 2) & 3) * 8 + (to >> 5) * 4 + (to & 3)
    both = jnp.dot(
        (row == wanted).astype(both.dtype), both, preferred_element_type=jnp.float32
    ).astype(both.dtype)
    held[...] = both
    copies = [
        pltpu.make_async_copy(held, out_ref.at[peer], sent.at[peer])
        for peer in range(out_ref.shape[0])
    ]
    for copy in copies:
        copy.start()
    for copy in copies:
        copy.wait()


def spread(place, own, first, second, peers):
    rows, width = own.shape
    vmem = pl.BlockSpec(memory_space=pltpu.VMEM)
    return pl.pallas_call(
        spread_kernel,
        in_specs=[pl.BlockSpec(memory_space=pltpu.SMEM)] + [vmem] * 3,
        out_specs=pl.BlockSpec(memory_space=pl.ANY),
        scratch_shapes=[
            pltpu.VMEM((HALF * rows, width), jnp.bfloat16),
            pltpu.SemaphoreType.DMA((peers,)),
        ],
        out_shape=jax.ShapeDtypeStruct((peers, HALF * rows, width), jnp.bfloat16),
        compiler_params=pltpu.CompilerParams(vmem_limit_bytes=8 * 1024 * 1024),
        name="spread",
    )(place, own, first, second)


def plan_kernel(tiles, slots, place, meta, lists):
    stride = meta.shape[0] // 2
    core, deep = place[0], place[1]
    lists[0] = 0
    for side in range(2):
        base = side * stride

        def look(slot, carry, base=base, side=side):
            query_tile = meta[base + 2 * slot]
            near = (query_tile & 3) ^ deep

            @pl.when((near >> 1) == core)
            def _():
                count = lists[0] + 1
                lists[0] = count
                lists[count] = (
                    (query_tile & 1)
                    + 2 * (query_tile >> 2)
                    + 16 * (meta[base + 2 * slot + 1] + side * tiles)
                    + 256 * meta[base + 2 * slots + 2 * slot]
                    + 65536 * meta[base + 2 * slots + 2 * slot + 1]
                )

            return carry

        lax.fori_loop(0, meta[base + 4 * slots], look, 0)
    for extra in range(1, UNROLL):
        lists[lists[0] + extra] = 0


def plan(place, meta, tiles, slots):
    smem = pl.BlockSpec(memory_space=pltpu.SMEM)
    return pl.pallas_call(
        functools.partial(plan_kernel, tiles, slots),
        in_specs=[smem, smem],
        out_specs=smem,
        out_shape=jax.ShapeDtypeStruct((2 * slots + 1 + UNROLL,), jnp.int32),
        compiler_params=pltpu.CompilerParams(vmem_limit_bytes=1024 * 1024),
        name="plan",
    )(place, meta)


def align_kernel(scale, lists, q_ref, own_ref, other_ref, out_ref, scores, weights):
    total, _ = q_ref.shape
    width = own_ref.shape[0]
    group = HALF * TILE
    pieces = 2 * QUARTERS
    piece = TILE // pieces

    across = (((1,), (1,)), ((), ()))
    for first in range(0, total, group):
        weights[first : first + group, :] = jnp.zeros((group, 2 * width), weights.dtype)
        query = q_ref[first : first + group, :]
        for side, ref in enumerate((own_ref, other_ref)):
            for at in range(0, width, CHUNK):
                scores[first : first + group, side * width + at : side * width + at + CHUNK] = (
                    lax.dot_general(
                        query, ref[at : at + CHUNK, :], across, preferred_element_type=jnp.float32
                    )
                    * scale
                )

    place_in_tile = lax.broadcasted_iota(jnp.int32, (TILE, TILE), 0)
    rows = (
        ((place_in_tile >> 2) & 3) * 32
        + (place_in_tile >> 5) * 8
        + ((place_in_tile >> 4) & 1) * 4
        + (place_in_tile & 3)
    )
    cols = lax.broadcasted_iota(jnp.int32, (TILE, TILE), 1)

    def batch(index, carry):
        made = []
        for k in range(UNROLL):
            slot = lists[1 + index * UNROLL + k]
            first = ((slot >> 1) & 7) * group + (slot & 1) * piece
            at_rows = [
                pl.ds(pl.multiple_of(first + step * HALF * piece, piece), piece)
                for step in range(pieces)
            ]
            at_col = pl.ds(pl.multiple_of(((slot >> 4) & 15) * TILE, TILE), TILE)
            score = jnp.concatenate([scores[at_row, at_col] for at_row in at_rows])
            weight = pair_weight(score, rows, cols, (slot >> 8) & 255, slot >> 16)
            made.append((at_rows, at_col, weight))
        for at_rows, at_col, weight in made:
            for step, at_row in enumerate(at_rows):
                weights[at_row, at_col] += weight[step * piece : (step + 1) * piece].astype(
                    weights.dtype
                )
        return carry

    lax.fori_loop(0, (lists[0] + UNROLL - 1) // UNROLL, batch, 0)

    for first in range(0, total, group):
        weight = weights[first : first + group, :].astype(jnp.bfloat16)
        out_ref[first : first + group, :] = (
            jnp.dot(weight[:, :width], own_ref[...], preferred_element_type=jnp.float32)
            + jnp.dot(weight[:, width:], other_ref[...], preferred_element_type=jnp.float32)
        ).astype(out_ref.dtype)


def align(lists, queries, own, other):
    rows, width = queries.shape
    columns = 2 * own.shape[0]
    smem = pl.BlockSpec(memory_space=pltpu.SMEM)
    vmem = pl.BlockSpec(memory_space=pltpu.VMEM)
    return pl.pallas_call(
        functools.partial(align_kernel, width ** (-0.5)),
        in_specs=[smem, vmem, vmem, vmem],
        out_specs=vmem,
        scratch_shapes=[
            pltpu.VMEM((rows, columns), jnp.float32),
            pltpu.VMEM((rows, columns), jnp.bfloat16),
        ],
        out_shape=jax.ShapeDtypeStruct((rows, width), jnp.bfloat16),
        compiler_params=pltpu.CompilerParams(vmem_limit_bytes=24 * 1024 * 1024),
        cost_estimate=pl.CostEstimate(
            flops=4 * rows * columns * width, bytes_accessed=0, transcendentals=0
        ),
        name="align",
    )(lists, queries, own, other)


def combine_kernel(cores, place, parts_ref, out_ref):
    peers, rows, _ = parts_ref.shape
    deep = place[1]
    for core in range(cores):
        total = sum(
            parts_ref[peer].astype(jnp.float32) for peer in range(core, peers, cores)
        ).astype(out_ref.dtype)
        out_ref[pl.ds(pl.multiple_of((core ^ (deep >> 1)) * rows, rows), rows), :] = total


def combine(place, parts, cores):
    peers, rows, width = parts.shape
    vmem = pl.BlockSpec(memory_space=pltpu.VMEM)
    return pl.pallas_call(
        functools.partial(combine_kernel, cores),
        in_specs=[pl.BlockSpec(memory_space=pltpu.SMEM), vmem],
        out_specs=vmem,
        out_shape=jax.ShapeDtypeStruct((cores * rows, width), jnp.bfloat16),
        compiler_params=pltpu.CompilerParams(vmem_limit_bytes=24 * 1024 * 1024),
        cost_estimate=pl.CostEstimate(
            flops=peers * rows * width, bytes_accessed=0, transcendentals=0
        ),
        name="combine",
    )(place, parts)


def sibling(value):
    return lax.ppermute(value, "c", [(0, 1), (1, 0)])


def on_device(queries, database, pair_tiles, pair_lengths, live_pairs):
    tile, width = queries.shape
    slots = pair_tiles.shape[1]
    core = lax.axis_index("c").astype(jnp.int32)
    deep = lax.axis_index("zh").astype(jnp.int32)
    place = jnp.stack([core, deep])
    places = lax.axis_size("zh")

    quarter = queries.reshape(lax.axis_size("yq"), 2, 2, 8, width)
    quarter = lax.dynamic_index_in_dim(quarter, lax.axis_index("yp"), 1, keepdims=False)
    quarter = lax.dynamic_index_in_dim(quarter, lax.axis_index("zl"), 1, keepdims=False)
    quarter = quarter.reshape(tile // QUARTERS, width)
    near = [(2 * z + c, 2 * (z ^ (1 + c)) + c) for z in range(places) for c in range(2)]
    far = [(2 * z + 1, 2 * (z ^ 3) + 1) for z in range(places)]
    first = lax.ppermute(quarter, ("zh", "c"), near)
    second = lax.ppermute(quarter, ("zh", "c"), far)

    own_meta = jnp.concatenate([pair_tiles.reshape(-1), pair_lengths.reshape(-1), live_pairs])
    own_meta = jnp.pad(own_meta, (0, 128 - own_meta.shape[0]))
    meta = jnp.concatenate([own_meta, sibling(own_meta)])
    lists = plan(place, meta, database.shape[0] // tile, slots)

    around = ("x", "yp", "zl")
    peers = math.prod(lax.axis_size(axis) for axis in around)
    panel = spread(place, quarter, first, second, peers)
    panel, database = lax.optimization_barrier((panel, database))
    other = sibling(database)
    panels = lax.all_to_all(panel, around, 0, 0, tiled=True).reshape(-1, width)

    terms = align(lists, panels, database, other)

    around = ("x", "yp", "zl", "c")
    peers = math.prod(lax.axis_size(axis) for axis in around)
    parts = lax.all_to_all(terms.reshape(peers, -1, width), around, 0, 0, tiled=True)
    column = combine(place, parts, lax.axis_size("c"))
    pieces = lax.all_to_all(column.reshape(-1, 4, width), ("zh", "yq"), 0, 0, tiled=True)
    return jnp.sum(pieces.astype(jnp.float32), axis=0).astype(jnp.bfloat16)


def solution(mesh):
    fine = Mesh(mesh.devices.reshape(4, 4, 4, 2, 2, 2), BLK + SHARD)
    both = BLK + SHARD
    in_specs = (P(BLK, None), P(both, None), P(both, None, None), P(both, None, None), P(both))
    return jax.shard_map(
        on_device, mesh=fine, in_specs=in_specs, out_specs=P(both, None), check_vma=False
    )
```

```python
import functools
import math

import jax
import jax.numpy as jnp
from jax import lax
from jax.experimental import pallas as pl
from jax.experimental.pallas import tpu as pltpu
from jax.sharding import Mesh
from jax.sharding import PartitionSpec as P

TILE = 128
BLK = ("x", "zh")
SHARD = ("yq", "yp", "zl", "c")
QUARTERS = 4
HALF = 2
CHUNK = 256
UNROLL = 4


def pair_weight(scores, rows, cols, row_count, col_count):
    valid = (rows < row_count) & (cols < col_count)
    masked = jnp.where(valid, scores, -1e30)
    row_max = jnp.max(masked, axis=1, keepdims=True)
    row_lse = row_max + jnp.log(jnp.sum(jnp.exp(masked - row_max), axis=1, keepdims=True))
    col_max = jnp.max(masked, axis=0, keepdims=True)
    col_lse = col_max + jnp.log(jnp.sum(jnp.exp(masked - col_max), axis=0, keepdims=True))
    weight = jnp.where(valid, jnp.exp(scores - 0.5 * (row_lse + col_lse)), 0.0)
    return weight.astype(jnp.bfloat16)


def spread_kernel(rows_ref, out_ref, held, sent):
    count = rows_ref.shape[0]
    to = lax.broadcasted_iota(jnp.int32, (count, count), 0)
    row = lax.broadcasted_iota(jnp.int32, (count, count), 1)
    wanted = ((to >> 2) & 3) * 16 + (to >> 4) * 4 + (to & 3)
    both = jnp.dot(
        (row == wanted).astype(rows_ref.dtype), rows_ref[...], preferred_element_type=jnp.float32
    ).astype(rows_ref.dtype)
    held[...] = both
    copies = [
        pltpu.make_async_copy(held, out_ref.at[peer], sent.at[peer])
        for peer in range(out_ref.shape[0])
    ]
    for copy in copies:
        copy.start()
    for copy in copies:
        copy.wait()


def spread(rows, peers):
    return pl.pallas_call(
        spread_kernel,
        in_specs=[pl.BlockSpec(memory_space=pltpu.VMEM)],
        out_specs=pl.BlockSpec(memory_space=pl.ANY),
        scratch_shapes=[
            pltpu.VMEM(rows.shape, jnp.bfloat16),
            pltpu.SemaphoreType.DMA((peers,)),
        ],
        out_shape=jax.ShapeDtypeStruct((peers, *rows.shape), jnp.bfloat16),
        compiler_params=pltpu.CompilerParams(vmem_limit_bytes=8 * 1024 * 1024),
        name="spread",
    )(rows)


def plan_kernel(tiles, slots, place, meta, lists):
    stride = meta.shape[0] // 2
    core, deep = place[0], place[1]
    lists[0] = 0
    for side in range(2):
        base = side * stride

        def look(slot, carry, base=base, side=side):
            query_tile = meta[base + 2 * slot]
            near = (query_tile & 3) ^ deep

            @pl.when((near >> 1) == core)
            def _():
                count = lists[0] + 1
                lists[0] = count
                lists[count] = (
                    (query_tile & 1)
                    + 2 * (query_tile >> 2)
                    + 16 * (meta[base + 2 * slot + 1] + side * tiles)
                    + 256 * meta[base + 2 * slots + 2 * slot]
                    + 65536 * meta[base + 2 * slots + 2 * slot + 1]
                    + 16777216 * (near & 1)
                )

            return carry

        lax.fori_loop(0, meta[base + 4 * slots], look, 0)
    for extra in range(1, UNROLL):
        lists[lists[0] + extra] = 0


def plan(place, meta, tiles, slots):
    smem = pl.BlockSpec(memory_space=pltpu.SMEM)
    return pl.pallas_call(
        functools.partial(plan_kernel, tiles, slots),
        in_specs=[smem, smem],
        out_specs=smem,
        out_shape=jax.ShapeDtypeStruct((2 * slots + 1 + UNROLL,), jnp.int32),
        compiler_params=pltpu.CompilerParams(vmem_limit_bytes=1024 * 1024),
        name="plan",
    )(place, meta)


def align_kernel(scale, lists, q_ref, own_ref, other_ref, out_ref, scores, weights):
    total, _ = q_ref.shape
    width = own_ref.shape[0]
    group = HALF * TILE
    pieces = 2 * QUARTERS
    piece = TILE // pieces

    across = (((1,), (1,)), ((), ()))
    for first in range(0, total, group):
        weights[first : first + group, :] = jnp.zeros((group, 2 * width), weights.dtype)
        query = q_ref[first : first + group, :]
        for side, ref in enumerate((own_ref, other_ref)):
            for at in range(0, width, CHUNK):
                scores[first : first + group, side * width + at : side * width + at + CHUNK] = (
                    lax.dot_general(
                        query, ref[at : at + CHUNK, :], across, preferred_element_type=jnp.float32
                    )
                    * scale
                )

    place_in_tile = lax.broadcasted_iota(jnp.int32, (TILE, TILE), 0)
    rows = (
        ((place_in_tile >> 2) & 3) * 32
        + (place_in_tile >> 5) * 8
        + ((place_in_tile >> 4) & 1) * 4
        + (place_in_tile & 3)
    )
    cols = lax.broadcasted_iota(jnp.int32, (TILE, TILE), 1)

    def batch(index, carry):
        made = []
        for k in range(UNROLL):
            slot = lists[1 + index * UNROLL + k]
            start = ((slot >> 1) & 7) * group
            scored = [
                pl.ds(pl.multiple_of(start + pair * TILE + (slot >> 24) * 64, 64), 64)
                for pair in range(2)
            ]
            first = start + (slot & 1) * piece
            at_rows = [
                pl.ds(pl.multiple_of(first + step * HALF * piece, piece), piece)
                for step in range(pieces)
            ]
            at_col = pl.ds(pl.multiple_of(((slot >> 4) & 15) * TILE, TILE), TILE)
            score = jnp.concatenate([scores[at_row, at_col] for at_row in scored])
            weight = pair_weight(score, rows, cols, (slot >> 8) & 255, (slot >> 16) & 255)
            made.append((at_rows, at_col, weight))
        for at_rows, at_col, weight in made:
            for step, at_row in enumerate(at_rows):
                weights[at_row, at_col] += weight[step * piece : (step + 1) * piece].astype(
                    weights.dtype
                )
        return carry

    lax.fori_loop(0, (lists[0] + UNROLL - 1) // UNROLL, batch, 0)

    for first in range(0, total, group):
        weight = weights[first : first + group, :].astype(jnp.bfloat16)
        out_ref[first : first + group, :] = (
            jnp.dot(weight[:, :width], own_ref[...], preferred_element_type=jnp.float32)
            + jnp.dot(weight[:, width:], other_ref[...], preferred_element_type=jnp.float32)
        ).astype(out_ref.dtype)


def align(lists, queries, own, other):
    rows, width = queries.shape
    columns = 2 * own.shape[0]
    smem = pl.BlockSpec(memory_space=pltpu.SMEM)
    vmem = pl.BlockSpec(memory_space=pltpu.VMEM)
    return pl.pallas_call(
        functools.partial(align_kernel, width ** (-0.5)),
        in_specs=[smem, vmem, vmem, vmem],
        out_specs=vmem,
        scratch_shapes=[
            pltpu.VMEM((rows, columns), jnp.float32),
            pltpu.VMEM((rows, columns), jnp.bfloat16),
        ],
        out_shape=jax.ShapeDtypeStruct((rows, width), jnp.bfloat16),
        compiler_params=pltpu.CompilerParams(vmem_limit_bytes=24 * 1024 * 1024),
        cost_estimate=pl.CostEstimate(
            flops=4 * rows * columns * width, bytes_accessed=0, transcendentals=0
        ),
        name="align",
    )(lists, queries, own, other)


def combine_kernel(cores, place, parts_ref, out_ref):
    peers, rows, _ = parts_ref.shape
    deep = place[1]
    for core in range(cores):
        total = sum(
            parts_ref[peer].astype(jnp.float32) for peer in range(core, peers, cores)
        ).astype(out_ref.dtype)
        out_ref[pl.ds(pl.multiple_of((core ^ (deep >> 1)) * rows, rows), rows), :] = total


def combine(place, parts, cores):
    peers, rows, width = parts.shape
    vmem = pl.BlockSpec(memory_space=pltpu.VMEM)
    return pl.pallas_call(
        functools.partial(combine_kernel, cores),
        in_specs=[pl.BlockSpec(memory_space=pltpu.SMEM), vmem],
        out_specs=vmem,
        out_shape=jax.ShapeDtypeStruct((cores * rows, width), jnp.bfloat16),
        compiler_params=pltpu.CompilerParams(vmem_limit_bytes=24 * 1024 * 1024),
        cost_estimate=pl.CostEstimate(
            flops=peers * rows * width, bytes_accessed=0, transcendentals=0
        ),
        name="combine",
    )(place, parts)


def sibling(value):
    return lax.ppermute(value, "c", [(0, 1), (1, 0)])


def on_device(queries, database, pair_tiles, pair_lengths, live_pairs):
    tile, width = queries.shape
    slots = pair_tiles.shape[1]
    core = lax.axis_index("c").astype(jnp.int32)
    deep = lax.axis_index("zh").astype(jnp.int32)
    place = jnp.stack([core, deep])

    half = queries.reshape(lax.axis_size("yq"), 2, 16, width)
    half = lax.dynamic_index_in_dim(half, lax.axis_index("yp"), 1, keepdims=False)
    half = half.reshape(tile // 2, width)
    route = [
        ((4 * (z ^ (2 * c + low)) + 2 * low + c), 4 * z + 2 * low + c)
        for z in range(lax.axis_size("zh"))
        for low in range(2)
        for c in range(2)
    ]
    fetched = lax.ppermute(half, ("zh", "zl", "c"), route)

    own_meta = jnp.concatenate([pair_tiles.reshape(-1), pair_lengths.reshape(-1), live_pairs])
    own_meta = jnp.pad(own_meta, (0, 128 - own_meta.shape[0]))
    meta = jnp.concatenate([own_meta, sibling(own_meta)])
    lists = plan(place, meta, database.shape[0] // tile, slots)

    around = ("x", "yp", "zl")
    peers = math.prod(lax.axis_size(axis) for axis in around)
    panel = spread(fetched, peers)
    panel, database = lax.optimization_barrier((panel, database))
    other = sibling(database)
    panels = lax.all_to_all(panel, around, 0, 0, tiled=True).reshape(-1, width)

    terms = align(lists, panels, database, other)

    around = ("x", "yp", "zl", "c")
    peers = math.prod(lax.axis_size(axis) for axis in around)
    parts = lax.all_to_all(terms.reshape(peers, -1, width), around, 0, 0, tiled=True)
    column = combine(place, parts, lax.axis_size("c"))
    pieces = lax.all_to_all(column.reshape(-1, 4, width), ("zh", "yq"), 0, 0, tiled=True)
    return jnp.sum(pieces.astype(jnp.float32), axis=0).astype(jnp.bfloat16)


def solution(mesh):
    fine = Mesh(mesh.devices.reshape(4, 4, 4, 2, 2, 2), BLK + SHARD)
    both = BLK + SHARD
    in_specs = (P(BLK, None), P(both, None), P(both, None, None), P(both, None, None), P(both))
    return jax.shard_map(
        on_device, mesh=fine, in_specs=in_specs, out_specs=P(both, None), check_vma=False
    )
```

```python
import functools
import math

import jax
import jax.numpy as jnp
from jax import lax
from jax.experimental import pallas as pl
from jax.experimental.pallas import tpu as pltpu
from jax.sharding import Mesh
from jax.sharding import PartitionSpec as P

TILE = 128
BLK = ("x", "zh")
SHARD = ("yq", "yp", "zl", "c")
QUARTERS = 4
HALF = 2
CHUNK = 256
UNROLL = 4


def pair_weight(scores, rows, cols, row_count, col_count):
    valid = (rows < row_count) & (cols < col_count)
    masked = jnp.where(valid, scores, -1e30)
    row_max = jnp.max(masked, axis=1, keepdims=True)
    row_lse = row_max + jnp.log(jnp.sum(jnp.exp(masked - row_max), axis=1, keepdims=True))
    col_max = jnp.max(masked, axis=0, keepdims=True)
    col_lse = col_max + jnp.log(jnp.sum(jnp.exp(masked - col_max), axis=0, keepdims=True))
    weight = jnp.where(valid, jnp.exp(scores - 0.5 * (row_lse + col_lse)), 0.0)
    return weight.astype(jnp.bfloat16)


def spread_kernel(rows_ref, out_ref, held, sent):
    count = rows_ref.shape[0]
    to = lax.broadcasted_iota(jnp.int32, (count, count), 0)
    row = lax.broadcasted_iota(jnp.int32, (count, count), 1)
    wanted = ((to >> 2) & 3) * 16 + (to >> 4) * 4 + (to & 3)
    both = jnp.dot(
        (row == wanted).astype(rows_ref.dtype), rows_ref[...], preferred_element_type=jnp.float32
    ).astype(rows_ref.dtype)
    held[...] = both
    copies = [
        pltpu.make_async_copy(held, out_ref.at[peer], sent.at[peer])
        for peer in range(out_ref.shape[0])
    ]
    for copy in copies:
        copy.start()
    for copy in copies:
        copy.wait()


def spread(rows, peers):
    return pl.pallas_call(
        spread_kernel,
        in_specs=[pl.BlockSpec(memory_space=pltpu.VMEM)],
        out_specs=pl.BlockSpec(memory_space=pl.ANY),
        scratch_shapes=[
            pltpu.VMEM(rows.shape, jnp.bfloat16),
            pltpu.SemaphoreType.DMA((peers,)),
        ],
        out_shape=jax.ShapeDtypeStruct((peers, *rows.shape), jnp.bfloat16),
        compiler_params=pltpu.CompilerParams(vmem_limit_bytes=8 * 1024 * 1024),
        name="spread",
    )(rows)


def plan_kernel(tiles, slots, place, meta, lists):
    stride = meta.shape[0] // 2
    core, deep = place[0], place[1]
    lists[0] = 0
    for side in range(2):
        base = side * stride

        def look(slot, carry, base=base, side=side):
            query_tile = meta[base + 2 * slot]
            near = (query_tile & 3) ^ deep

            @pl.when((near >> 1) == core)
            def _():
                count = lists[0] + 1
                lists[0] = count
                lists[count] = (
                    (query_tile & 1)
                    + 2 * (query_tile >> 2)
                    + 16 * (meta[base + 2 * slot + 1] + side * tiles)
                    + 256 * meta[base + 2 * slots + 2 * slot]
                    + 65536 * meta[base + 2 * slots + 2 * slot + 1]
                    + 16777216 * (near & 1)
                )

            return carry

        lax.fori_loop(0, meta[base + 4 * slots], look, 0)
    for extra in range(1, UNROLL):
        lists[lists[0] + extra] = 0


def plan(place, meta, tiles, slots):
    smem = pl.BlockSpec(memory_space=pltpu.SMEM)
    return pl.pallas_call(
        functools.partial(plan_kernel, tiles, slots),
        in_specs=[smem, smem],
        out_specs=smem,
        out_shape=jax.ShapeDtypeStruct((2 * slots + 1 + UNROLL,), jnp.int32),
        compiler_params=pltpu.CompilerParams(vmem_limit_bytes=1024 * 1024),
        name="plan",
    )(place, meta)


def align_kernel(scale, lists, q_ref, own_ref, other_ref, out_ref, scores, weights):
    total, _ = q_ref.shape
    width = own_ref.shape[0]
    group = HALF * TILE
    pieces = 2 * QUARTERS
    piece = TILE // pieces

    across = (((1,), (1,)), ((), ()))
    for first in range(0, total, group):
        weights[first : first + group, :] = jnp.zeros((group, 2 * width), weights.dtype)
        query = jnp.concatenate(
            [
                q_ref[block * 64 : (block + 1) * 64, :]
                for block in range(first // group, total // 64, total // group)
            ]
        )
        for side, ref in enumerate((own_ref, other_ref)):
            for at in range(0, width, CHUNK):
                scores[first : first + group, side * width + at : side * width + at + CHUNK] = (
                    lax.dot_general(
                        query, ref[at : at + CHUNK, :], across, preferred_element_type=jnp.float32
                    )
                    * scale
                )

    place_in_tile = lax.broadcasted_iota(jnp.int32, (TILE, TILE), 0)
    rows = (
        ((place_in_tile >> 2) & 3) * 32
        + (place_in_tile >> 5) * 8
        + ((place_in_tile >> 4) & 1) * 4
        + (place_in_tile & 3)
    )
    cols = lax.broadcasted_iota(jnp.int32, (TILE, TILE), 1)

    def batch(index, carry):
        made = []
        for k in range(UNROLL):
            slot = lists[1 + index * UNROLL + k]
            start = ((slot >> 1) & 7) * group
            scored = [
                pl.ds(pl.multiple_of(start + pair * TILE + (slot >> 24) * 64, 64), 64)
                for pair in range(2)
            ]
            first = start + (slot & 1) * piece
            at_rows = [
                pl.ds(pl.multiple_of(first + step * HALF * piece, piece), piece)
                for step in range(pieces)
            ]
            at_col = pl.ds(pl.multiple_of(((slot >> 4) & 15) * TILE, TILE), TILE)
            score = jnp.concatenate([scores[at_row, at_col] for at_row in scored])
            weight = pair_weight(score, rows, cols, (slot >> 8) & 255, (slot >> 16) & 255)
            made.append((at_rows, at_col, weight))
        for at_rows, at_col, weight in made:
            for step, at_row in enumerate(at_rows):
                weights[at_row, at_col] += weight[step * piece : (step + 1) * piece].astype(
                    weights.dtype
                )
        return carry

    lax.fori_loop(0, (lists[0] + UNROLL - 1) // UNROLL, batch, 0)

    groups = total // group
    sent = 2 * piece
    for index in range(groups):
        terms = (
            jnp.dot(
                weights[index * group : (index + 1) * group, :width],
                own_ref[...],
                preferred_element_type=jnp.float32,
            )
            + jnp.dot(
                weights[index * group : (index + 1) * group, width:],
                other_ref[...],
                preferred_element_type=jnp.float32,
            )
        ).astype(out_ref.dtype)
        for peer in range(group // sent):
            at = (peer * groups + index) * sent
            out_ref[at : at + sent, :] = terms[peer * sent : (peer + 1) * sent]


def align(lists, queries, own, other):
    rows, width = queries.shape
    columns = 2 * own.shape[0]
    smem = pl.BlockSpec(memory_space=pltpu.SMEM)
    vmem = pl.BlockSpec(memory_space=pltpu.VMEM)
    return pl.pallas_call(
        functools.partial(align_kernel, width ** (-0.5)),
        in_specs=[smem, vmem, vmem, vmem],
        out_specs=vmem,
        scratch_shapes=[
            pltpu.VMEM((rows, columns), jnp.float32),
            pltpu.VMEM((rows, columns), jnp.bfloat16),
        ],
        out_shape=jax.ShapeDtypeStruct((rows, width), jnp.bfloat16),
        compiler_params=pltpu.CompilerParams(vmem_limit_bytes=24 * 1024 * 1024),
        cost_estimate=pl.CostEstimate(
            flops=4 * rows * columns * width, bytes_accessed=0, transcendentals=0
        ),
        name="align",
    )(lists, queries, own, other)


def combine_kernel(cores, groups, place, parts_ref, out_ref):
    peers, rows, _ = parts_ref.shape
    deep = place[1]
    for core in range(cores):
        total = sum(
            parts_ref[peer].astype(jnp.float32)
            for peer in range(peers)
            if peer // groups % cores == core
        ).astype(out_ref.dtype)
        out_ref[pl.ds(pl.multiple_of((core ^ (deep >> 1)) * rows, rows), rows), :] = total


def combine(place, parts, cores, groups):
    peers, rows, width = parts.shape
    vmem = pl.BlockSpec(memory_space=pltpu.VMEM)
    return pl.pallas_call(
        functools.partial(combine_kernel, cores, groups),
        in_specs=[pl.BlockSpec(memory_space=pltpu.SMEM), vmem],
        out_specs=vmem,
        out_shape=jax.ShapeDtypeStruct((cores * rows, width), jnp.bfloat16),
        compiler_params=pltpu.CompilerParams(vmem_limit_bytes=24 * 1024 * 1024),
        cost_estimate=pl.CostEstimate(
            flops=peers * rows * width, bytes_accessed=0, transcendentals=0
        ),
        name="combine",
    )(place, parts)


def sibling(value):
    return lax.ppermute(value, "c", [(0, 1), (1, 0)])


def on_device(queries, database, pair_tiles, pair_lengths, live_pairs):
    tile, width = queries.shape
    slots = pair_tiles.shape[1]
    core = lax.axis_index("c").astype(jnp.int32)
    deep = lax.axis_index("zh").astype(jnp.int32)
    place = jnp.stack([core, deep])

    half = queries.reshape(lax.axis_size("yq"), 2, 16, width)
    half = lax.dynamic_index_in_dim(half, lax.axis_index("yp"), 1, keepdims=False)
    half = half.reshape(tile // 2, width)
    route = [
        ((4 * (z ^ (2 * c + low)) + 2 * low + c), 4 * z + 2 * low + c)
        for z in range(lax.axis_size("zh"))
        for low in range(2)
        for c in range(2)
    ]
    fetched = lax.ppermute(half, ("zh", "zl", "c"), route)

    own_meta = jnp.concatenate([pair_tiles.reshape(-1), pair_lengths.reshape(-1), live_pairs])
    own_meta = jnp.pad(own_meta, (0, 128 - own_meta.shape[0]))
    meta = jnp.concatenate([own_meta, sibling(own_meta)])
    lists = plan(place, meta, database.shape[0] // tile, slots)

    around = ("yp", "zl", "x")
    peers = math.prod(lax.axis_size(axis) for axis in around)
    panel = spread(fetched, peers)
    panel, database = lax.optimization_barrier((panel, database))
    other = sibling(database)
    panels = lax.all_to_all(panel, around, 0, 0, tiled=True).reshape(-1, width)

    terms = align(lists, panels, database, other)

    around = ("yp", "zl", "c", "x")
    peers = math.prod(lax.axis_size(axis) for axis in around)
    parts = lax.all_to_all(terms.reshape(peers, -1, width), around, 0, 0, tiled=True)
    column = combine(place, parts, lax.axis_size("c"), lax.axis_size("x"))
    pieces = lax.all_to_all(column.reshape(-1, 4, width), ("zh", "yq"), 0, 0, tiled=True)
    return jnp.sum(pieces.astype(jnp.float32), axis=0).astype(jnp.bfloat16)


def solution(mesh):
    fine = Mesh(mesh.devices.reshape(4, 4, 4, 2, 2, 2), BLK + SHARD)
    both = BLK + SHARD
    in_specs = (P(BLK, None), P(both, None), P(both, None, None), P(both, None, None), P(both))
    return jax.shard_map(
        on_device, mesh=fine, in_specs=in_specs, out_specs=P(both, None), check_vma=False
    )
```

```python
import functools
import math

import jax
import jax.numpy as jnp
from jax import lax
from jax.experimental import pallas as pl
from jax.experimental.pallas import tpu as pltpu
from jax.sharding import Mesh
from jax.sharding import PartitionSpec as P

TILE = 128
BLK = ("x", "zh")
SHARD = ("yq", "yp", "zl", "c")
QUARTERS = 4
HALF = 2
CHUNK = 256
UNROLL = 4


def pair_weight(scores, rows, cols, row_count, col_count):
    valid = (rows < row_count) & (cols < col_count)
    masked = jnp.where(valid, scores, -1e30)
    row_max = jnp.max(masked, axis=1, keepdims=True)
    row_lse = row_max + jnp.log(jnp.sum(jnp.exp(masked - row_max), axis=1, keepdims=True))
    col_max = jnp.max(masked, axis=0, keepdims=True)
    col_lse = col_max + jnp.log(jnp.sum(jnp.exp(masked - col_max), axis=0, keepdims=True))
    weight = jnp.where(valid, jnp.exp(scores - 0.5 * (row_lse + col_lse)), 0.0)
    return weight.astype(jnp.bfloat16)


def spread_kernel(rows_ref, out_ref, held, sent):
    count = rows_ref.shape[0]
    to = lax.broadcasted_iota(jnp.int32, (count, count), 0)
    row = lax.broadcasted_iota(jnp.int32, (count, count), 1)
    wanted = ((to >> 2) & 3) * 16 + (to >> 4) * 4 + (to & 3)
    both = jnp.dot(
        (row == wanted).astype(rows_ref.dtype), rows_ref[...], preferred_element_type=jnp.float32
    ).astype(rows_ref.dtype)
    held[...] = both
    copies = [
        pltpu.make_async_copy(held, out_ref.at[peer], sent.at[peer])
        for peer in range(out_ref.shape[0])
    ]
    for copy in copies:
        copy.start()
    for copy in copies:
        copy.wait()


def spread(rows, peers):
    return pl.pallas_call(
        spread_kernel,
        in_specs=[pl.BlockSpec(memory_space=pltpu.VMEM)],
        out_specs=pl.BlockSpec(memory_space=pl.ANY),
        scratch_shapes=[
            pltpu.VMEM(rows.shape, jnp.bfloat16),
            pltpu.SemaphoreType.DMA((peers,)),
        ],
        out_shape=jax.ShapeDtypeStruct((peers, *rows.shape), jnp.bfloat16),
        compiler_params=pltpu.CompilerParams(vmem_limit_bytes=8 * 1024 * 1024),
        name="spread",
    )(rows)


def plan_kernel(tiles, slots, place, meta, lists):
    stride = meta.shape[0] // 2
    core, deep = place[0], place[1]
    last = lists.shape[0] - 1
    lists[0] = 0
    lists[last] = 0
    for side in range(2):
        base = side * stride

        def look(slot, carry, base=base, side=side):
            query_tile = meta[base + 2 * slot]
            near = (query_tile & 3) ^ deep

            @pl.when((near >> 1) == core)
            def _():
                count = lists[0] + 1
                lists[0] = count
                column = meta[base + 2 * slot + 1] + side * tiles
                block = (query_tile >> 2) * tiles + (column >> 1)
                lists[last] = lists[last] | jnp.left_shift(jnp.int32(1), block)
                lists[count] = (
                    (query_tile & 1)
                    + 2 * (query_tile >> 2)
                    + 16 * (meta[base + 2 * slot + 1] + side * tiles)
                    + 256 * meta[base + 2 * slots + 2 * slot]
                    + 65536 * meta[base + 2 * slots + 2 * slot + 1]
                    + 16777216 * (near & 1)
                )

            return carry

        lax.fori_loop(0, meta[base + 4 * slots], look, 0)
    for extra in range(1, UNROLL):
        lists[lists[0] + extra] = 0


def plan(place, meta, tiles, slots):
    smem = pl.BlockSpec(memory_space=pltpu.SMEM)
    return pl.pallas_call(
        functools.partial(plan_kernel, tiles, slots),
        in_specs=[smem, smem],
        out_specs=smem,
        out_shape=jax.ShapeDtypeStruct((2 * slots + 2 + UNROLL,), jnp.int32),
        compiler_params=pltpu.CompilerParams(vmem_limit_bytes=1024 * 1024),
        name="plan",
    )(place, meta)


def align_kernel(scale, lists, q_ref, own_ref, other_ref, out_ref, scores, weights):
    total, _ = q_ref.shape
    width = own_ref.shape[0]
    group = HALF * TILE
    pieces = 2 * QUARTERS
    piece = TILE // pieces

    across = (((1,), (1,)), ((), ()))
    weights[...] = jnp.zeros_like(weights)
    used = lists[lists.shape[0] - 1]
    chunks = 2 * width // CHUNK
    for index in range(total // group):
        part = slice(index * group, (index + 1) * group)
        for chunk in range(chunks):
            ref = own_ref if chunk < chunks // 2 else other_ref
            at = chunk % (chunks // 2) * CHUNK

            @pl.when(((used >> (index * chunks + chunk)) & 1) == 1)
            def _(part=part, chunk=chunk, ref=ref, at=at):
                scores[part, chunk * CHUNK : (chunk + 1) * CHUNK] = (
                    lax.dot_general(
                        q_ref[part, :], ref[at : at + CHUNK, :], across,
                        preferred_element_type=jnp.float32,
                    )
                    * scale
                )

    place_in_tile = lax.broadcasted_iota(jnp.int32, (TILE, TILE), 0)
    rows = (
        ((place_in_tile >> 2) & 3) * 32
        + (place_in_tile >> 5) * 8
        + ((place_in_tile >> 4) & 1) * 4
        + (place_in_tile & 3)
    )
    cols = lax.broadcasted_iota(jnp.int32, (TILE, TILE), 1)

    def batch(index, carry):
        made = []
        for k in range(UNROLL):
            slot = lists[1 + index * UNROLL + k]
            start = ((slot >> 1) & 7) * group
            scored = [
                pl.ds(pl.multiple_of(start + pair * TILE + (slot >> 24) * 64, 64), 64)
                for pair in range(2)
            ]
            first = start + (slot & 1) * piece
            at_rows = [
                pl.ds(pl.multiple_of(first + step * HALF * piece, piece), piece)
                for step in range(pieces)
            ]
            at_col = pl.ds(pl.multiple_of(((slot >> 4) & 15) * TILE, TILE), TILE)
            score = jnp.concatenate([scores[at_row, at_col] for at_row in scored])
            weight = pair_weight(score, rows, cols, (slot >> 8) & 255, (slot >> 16) & 255)
            made.append((at_rows, at_col, weight))
        for at_rows, at_col, weight in made:
            for step, at_row in enumerate(at_rows):
                weights[at_row, at_col] += weight[step * piece : (step + 1) * piece].astype(
                    weights.dtype
                )
        return carry

    lax.fori_loop(0, (lists[0] + UNROLL - 1) // UNROLL, batch, 0)

    for first in range(0, total, group):
        weight = weights[first : first + group, :].astype(jnp.bfloat16)
        out_ref[first : first + group, :] = (
            jnp.dot(weight[:, :width], own_ref[...], preferred_element_type=jnp.float32)
            + jnp.dot(weight[:, width:], other_ref[...], preferred_element_type=jnp.float32)
        ).astype(out_ref.dtype)


def align(lists, queries, own, other):
    rows, width = queries.shape
    columns = 2 * own.shape[0]
    smem = pl.BlockSpec(memory_space=pltpu.SMEM)
    vmem = pl.BlockSpec(memory_space=pltpu.VMEM)
    return pl.pallas_call(
        functools.partial(align_kernel, width ** (-0.5)),
        in_specs=[smem, vmem, vmem, vmem],
        out_specs=vmem,
        scratch_shapes=[
            pltpu.VMEM((rows, columns), jnp.float32),
            pltpu.VMEM((rows, columns), jnp.bfloat16),
        ],
        out_shape=jax.ShapeDtypeStruct((rows, width), jnp.bfloat16),
        compiler_params=pltpu.CompilerParams(vmem_limit_bytes=24 * 1024 * 1024),
        cost_estimate=pl.CostEstimate(
            flops=4 * rows * columns * width, bytes_accessed=0, transcendentals=0
        ),
        name="align",
    )(lists, queries, own, other)


def combine_kernel(cores, place, parts_ref, out_ref):
    peers, rows, _ = parts_ref.shape
    deep = place[1]
    for core in range(cores):
        total = sum(
            parts_ref[peer].astype(jnp.float32) for peer in range(core, peers, cores)
        ).astype(out_ref.dtype)
        out_ref[pl.ds(pl.multiple_of((core ^ (deep >> 1)) * rows, rows), rows), :] = total


def combine(place, parts, cores):
    peers, rows, width = parts.shape
    vmem = pl.BlockSpec(memory_space=pltpu.VMEM)
    return pl.pallas_call(
        functools.partial(combine_kernel, cores),
        in_specs=[pl.BlockSpec(memory_space=pltpu.SMEM), vmem],
        out_specs=vmem,
        out_shape=jax.ShapeDtypeStruct((cores * rows, width), jnp.bfloat16),
        compiler_params=pltpu.CompilerParams(vmem_limit_bytes=24 * 1024 * 1024),
        cost_estimate=pl.CostEstimate(
            flops=peers * rows * width, bytes_accessed=0, transcendentals=0
        ),
        name="combine",
    )(place, parts)


def sibling(value):
    return lax.ppermute(value, "c", [(0, 1), (1, 0)])


def on_device(queries, database, pair_tiles, pair_lengths, live_pairs):
    tile, width = queries.shape
    slots = pair_tiles.shape[1]
    core = lax.axis_index("c").astype(jnp.int32)
    deep = lax.axis_index("zh").astype(jnp.int32)
    place = jnp.stack([core, deep])

    half = queries.reshape(lax.axis_size("yq"), 2, 16, width)
    half = lax.dynamic_index_in_dim(half, lax.axis_index("yp"), 1, keepdims=False)
    half = half.reshape(tile // 2, width)
    route = [
        ((4 * (z ^ (2 * c + low)) + 2 * low + c), 4 * z + 2 * low + c)
        for z in range(lax.axis_size("zh"))
        for low in range(2)
        for c in range(2)
    ]
    fetched = lax.ppermute(half, ("zh", "zl", "c"), route)

    own_meta = jnp.concatenate([pair_tiles.reshape(-1), pair_lengths.reshape(-1), live_pairs])
    own_meta = jnp.pad(own_meta, (0, 128 - own_meta.shape[0]))
    meta = jnp.concatenate([own_meta, sibling(own_meta)])
    lists = plan(place, meta, database.shape[0] // tile, slots)

    around = ("x", "yp", "zl")
    peers = math.prod(lax.axis_size(axis) for axis in around)
    panel = spread(fetched, peers)
    panel, database = lax.optimization_barrier((panel, database))
    other = sibling(database)
    panels = lax.all_to_all(panel, around, 0, 0, tiled=True).reshape(-1, width)

    terms = align(lists, panels, database, other)

    around = ("x", "yp", "zl", "c")
    peers = math.prod(lax.axis_size(axis) for axis in around)
    parts = lax.all_to_all(terms.reshape(peers, -1, width), around, 0, 0, tiled=True)
    column = combine(place, parts, lax.axis_size("c"))
    pieces = lax.all_to_all(column.reshape(-1, 4, width), ("zh", "yq"), 0, 0, tiled=True)
    return jnp.sum(pieces.astype(jnp.float32), axis=0).astype(jnp.bfloat16)


def solution(mesh):
    fine = Mesh(mesh.devices.reshape(4, 4, 4, 2, 2, 2), BLK + SHARD)
    both = BLK + SHARD
    in_specs = (P(BLK, None), P(both, None), P(both, None, None), P(both, None, None), P(both))
    return jax.shard_map(
        on_device, mesh=fine, in_specs=in_specs, out_specs=P(both, None), check_vma=False
    )
```
